32 devices in a mesh: groups: 2 (over x), dp: 16 (over z, y, core).
Axes of the slice: x: 2, y: 2, z: 4, core: 2. Of those that a mesh axis runs over, the one named last changes fastest.
Arguments:
- layer_inputs: bfloat16 [4096, 2048], P(('groups', 'dp')), parts along dimension 0, may hold values from -0.125 to 0.125
- output_grads: bfloat16 [4096, 8192], P(('groups', 'dp')), parts along dimension 0, may hold values from -0.0625 to 0.0625
- query_grads: bfloat16 [128, 2, 512, 256], P('dp'), may hold values from -6 to 6
- eigenvalues: float32 [128, 512, 256], P('dp'), may hold values from 0.01 to 900, as said below
- out_basis: bfloat16 [64, 128, 128], replicated, may hold values from -0.5 to 0.5
- in_basis: bfloat16 [16, 128, 128], replicated, may hold values from -0.5 to 0.5
- doc_lengths: int32 [32], P('groups'), parts along dimension 0, may hold values from 1 to 512, 2048 in all
Outputs:
- influence: float32 [32, 2], P(('groups', 'dp')), parts along dimension 0
The draws below stay inside these ranges and needn't reach their ends.
There are 2 independent parts, one for each index of `groups`. The reference program is written for one: setup_inputs(seed, part) draws one part's arguments, and reference() takes and returns one part's arrays. A program takes and returns all parts, laid end to end along the dimension named above; an argument that names none is the same for every part. Nothing has to cross between parts.
Inputs may be any that keep to these rules, and one draw needn't show every extreme that they name: `doc_lengths`: the 16 lengths sum to 2048, and the largest is exactly 512. `eigenvalues`: positive.
All inputs are finite; a program needn't handle non-finite values.
Results may differ from the reference program's by a relative error of at most 0.0044.
Values may be sent and summed in bfloat16 or wider, within the bound.
No kernel may reach another device: no remote copies, remote signals or barrier semaphores. Data moves between devices by JAX's collectives and lax.ppermute only.
A program may use at most 192 MiB of HBM per device.

```python
import math
import jax
import jax.numpy as jnp
import numpy as np
from jax import lax

DIN = 2048
DOUT = 8192
KB = 128
BO = 512
BI = 256
Q = 2
DOC_MAX = 512
NBLK = 128
TOKENS = 2048
DOCS = 16


def draw_eigenvalues(key, part):
    keys = jax.random.split(jax.random.fold_in(key, 17), 3)
    base = jnp.exp(jax.random.uniform(keys[0], (NBLK, BO, BI), jnp.float32, math.log(0.01), 0.0))
    top_factor = 3.0
    row_scale = jnp.exp(jax.random.uniform(keys[1], (NBLK, BO, 1), jnp.float32, 0.0, math.log(10.0)))
    col_scale = jnp.exp(jax.random.uniform(keys[2], (NBLK, 1, BI), jnp.float32, 0.0, math.log(10.0)))
    rising = 1.0 + (top_factor - 1.0) * jnp.arange(NBLK, dtype=jnp.float32)[:, None, None] / max(NBLK - 1, 1)
    return base * row_scale * col_scale * rising


def steps_of(rng, dims, cuts, low, high):
    level, own = 1.0, jax.random.fold_in(rng, 6)
    for dim, shards_of in cuts:
        draws = jnp.exp(jax.random.uniform(jax.random.fold_in(own, dim), (shards_of,), jnp.float32, low / len(cuts), high / len(cuts)))
        level = level * jnp.repeat(draws, dims[dim] // shards_of).reshape([-1 if axis == dim else 1 for axis in range(len(dims))])
    return level


def length_profile(number_of, total, most, slope):
    weights = [(1 << 20) // math.isqrt(rank ** slope) + 1 for rank in range(2, number_of + 1)]
    spare, given = total - most - (number_of - 1), [1] * (number_of - 1)
    while spare > 0:
        candidates = [i for i in range(number_of - 1) if given[i] < most]
        pool, budget = sum([weights[i] for i in candidates]), spare
        for i in candidates:
            addition = min(most - given[i], max(1, budget * weights[i] // pool), spare)
            given[i] = given[i] + addition
            spare = spare - addition
    return np.array([most] + given)


def ragged(stream_key, amount, total, limit, lean):
    if amount == 2:
        one = jax.random.randint(stream_key, (), max(1, total - limit), min(limit, total - 1) + 1)
        return jnp.stack([one, total - one])
    sizes = jnp.asarray(length_profile(amount, total, limit, lean), jnp.int32)
    couples = (amount - 1) // 2
    source_of, receiver = sizes[1:1 + 2 * couples:2], sizes[2:2 + 2 * couples:2]
    margin = jnp.minimum(source_of - 1, limit - receiver)
    moved = jax.random.randint(jax.random.fold_in(stream_key, 1), (couples,), 0, 1 << 20) % (margin + 1)
    sizes = sizes.at[1:1 + 2 * couples:2].set(source_of - moved).at[2:2 + 2 * couples:2].set(receiver + moved)
    return sizes[jax.random.permutation(jax.random.fold_in(stream_key, 2), amount)]


def normal_values(own_key, extent, deviation, bound, pieces=(), held_as=jnp.bfloat16):
    gain = steps_of(own_key, extent, pieces, -0.22, 0.18) if pieces else 1.0
    array = jax.random.normal(own_key, extent, jnp.float32) * deviation * gain
    return jnp.minimum(jnp.maximum(array, -bound), bound).astype(held_as)


def setup_inputs(seed: int = 0, part: int = 0) -> dict:
    splits = jax.random.split(jax.random.key(seed), 8)
    part_splits = jax.random.split(jax.random.fold_in(splits[7], part), 8)
    layer_inputs = normal_values(part_splits[0], (TOKENS, DIN), (DIN ** -0.5), 0.125, ((0, 16),))
    output_grads = normal_values(part_splits[1], (TOKENS, DOUT), (DOUT ** -0.5), 0.0625, ((0, 16),))
    query_grads = normal_values(splits[2], (NBLK, Q, BO, BI), 1.0, 6.0, ((0, 16),))
    eigenvalues = draw_eigenvalues(jax.random.fold_in(splits[7], 71), part)
    out_basis = normal_values(splits[4], (DOUT // KB, KB, KB), KB ** -0.5, 0.5)
    in_basis = normal_values(splits[5], (DIN // KB, KB, KB), KB ** -0.5, 0.5)
    doc_lengths = ragged(part_splits[6], DOCS, TOKENS, DOC_MAX, 2).astype(jnp.int32)
    return {"layer_inputs": layer_inputs, "output_grads": output_grads, "query_grads": query_grads, "eigenvalues": eigenvalues, "out_basis": out_basis, "in_basis": in_basis, "doc_lengths": doc_lengths}


def turn_rows(columns, basis_blocks):
    group_count = basis_blocks.shape[0]
    block_width = basis_blocks.shape[1]
    grouped = columns.reshape(columns.shape[0], group_count, block_width).astype(jnp.float32)
    turned = jnp.einsum('tnk,nkj->tnj', grouped, basis_blocks.astype(jnp.float32))
    return turned.reshape(columns.shape).astype(jnp.bfloat16)


def reference(layer_inputs, output_grads, query_grads, eigenvalues, out_basis, in_basis, doc_lengths):
    damping = 0.1 * jnp.mean(eigenvalues)
    rotated_grads = turn_rows(output_grads, out_basis)
    rotated_inputs = turn_rows(layer_inputs, in_basis)
    in_tiles = DIN // BI
    out_sets = out_basis.reshape(DOUT // BO, BO // KB, KB, KB)
    in_sets = in_basis.reshape(in_tiles, BI // KB, KB, KB)
    doc_ends = jnp.cumsum(doc_lengths).astype(jnp.int32)
    positions = jnp.arange(TOKENS, dtype=jnp.int32)
    doc_of = jnp.sum((positions[:, None] >= doc_ends[None, :]).astype(jnp.int32), axis=1).astype(jnp.int32)

    def one_tile(running, tile_index):
        out_id = (tile_index // in_tiles).astype(jnp.int32)
        in_id = (tile_index % in_tiles).astype(jnp.int32)
        grads = lax.dynamic_slice_in_dim(rotated_grads, (out_id * BO).astype(jnp.int32), BO, 1)
        inputs = lax.dynamic_slice_in_dim(rotated_inputs, (in_id * BI).astype(jnp.int32), BI, 1)
        tile_grads = lax.dynamic_index_in_dim(query_grads, tile_index, 0, keepdims=False)
        tile_eigen = lax.dynamic_index_in_dim(eigenvalues, tile_index, 0, keepdims=False)
        in_blocks = lax.dynamic_index_in_dim(in_sets, in_id, 0, keepdims=False)
        out_blocks = lax.dynamic_index_in_dim(out_sets, out_id, 0, keepdims=False)
        grouped = tile_grads.reshape(Q, BO, BI // KB, KB).astype(jnp.float32)
        half_turned = jnp.einsum('qonk,nkj->qonj', grouped, in_blocks.astype(jnp.float32))
        half_turned = half_turned.reshape(Q, BO, BI).astype(jnp.bfloat16)
        grouped = half_turned.reshape(Q, BO // KB, KB, BI).astype(jnp.float32)
        turned = jnp.einsum('qnki,nkj->qnji', grouped, out_blocks.astype(jnp.float32)).reshape(Q, BO, BI)
        preconditioned = (turned / (tile_eigen[None] + damping)).astype(jnp.bfloat16)
        projected = jnp.einsum('ti,qoi->tqo', inputs.astype(jnp.float32), preconditioned.astype(jnp.float32))
        return running + jnp.sum(projected * grads.astype(jnp.float32)[:, None, :], axis=2), None

    score, _ = lax.scan(one_tile, jnp.zeros((TOKENS, Q), jnp.float32), jnp.arange(NBLK, dtype=jnp.int32))
    return jax.ops.segment_sum(score, doc_of, num_segments=DOCS)
```

```python
import functools
import math

import jax
import jax.numpy as jnp
from jax import lax
from jax.experimental import pallas as pl
from jax.experimental.pallas import tpu as pltpu
from jax.sharding import PartitionSpec as P

VMEM_LIMIT = 48 * 1024 * 1024
F32 = jnp.float32
BF16 = jnp.bfloat16


def turn_rows(columns, basis_blocks):
    group_count = basis_blocks.shape[0]
    block_width = basis_blocks.shape[1]
    grouped = columns.reshape(columns.shape[0], group_count, block_width)
    turned = jnp.einsum("tnk,nkj->tnj", grouped, basis_blocks, preferred_element_type=jnp.float32)
    return turned.reshape(columns.shape).astype(jnp.bfloat16)


def precondition(query_grads, eigenvalues, damping, tile_out, tile_in):
    blocks, queries, rows_out, rows_in = query_grads.shape
    block_width = tile_in.shape[-1]
    grouped = query_grads.reshape(blocks, queries, rows_out, rows_in // block_width, block_width)
    half_turned = jnp.einsum(
        "bqonk,bnkj->bqonj", grouped, tile_in, preferred_element_type=jnp.float32
    )
    half_turned = half_turned.reshape(blocks, queries, rows_out, rows_in).astype(jnp.bfloat16)
    grouped = half_turned.reshape(blocks, queries, rows_out // block_width, block_width, rows_in)
    turned = jnp.einsum("bqnki,bnkj->bqnji", grouped, tile_out, preferred_element_type=jnp.float32)
    turned = turned.reshape(blocks, queries, rows_out, rows_in)
    return (turned / (eigenvalues[:, None] + damping)).astype(jnp.bfloat16)


def tally_scores(grads_got, inputs_got, preconditioned, doc_starts, doc_ends):
    blocks, total_rows, rows_out = grads_got.shape
    queries = preconditioned.shape[1]
    row_step = math.gcd(1024, total_rows)
    flat_pre = preconditioned.reshape(blocks, queries * rows_out, preconditioned.shape[3])

    def one_piece(running, piece_index):
        start_row = piece_index * row_step
        grads_piece = lax.dynamic_slice_in_dim(grads_got, start_row, row_step, 1)
        inputs_piece = lax.dynamic_slice_in_dim(inputs_got, start_row, row_step, 1)
        projected = jnp.einsum(
            "bti,bpi->btp", inputs_piece, flat_pre, preferred_element_type=jnp.float32
        )
        projected = projected.reshape(blocks, row_step, queries, rows_out)
        scores = jnp.sum(projected * grads_piece[:, :, None, :].astype(jnp.float32), axis=(0, 3))
        positions = start_row + lax.iota(jnp.int32, row_step)
        member = (
            (positions[:, None] >= doc_starts[None, :]) & (positions[:, None] < doc_ends[None, :])
        ).astype(jnp.float32)
        added = jnp.einsum("td,tq->dq", member, scores, precision=lax.Precision.HIGHEST)
        return (running + added, None)

    initial = jnp.zeros((doc_starts.shape[0], queries), jnp.float32)
    summed, _ = lax.scan(one_piece, initial, jnp.arange(total_rows // row_step, dtype=jnp.int32))
    return summed


def local_general(
    layer_inputs, output_grads, query_grads, eigenvalues, out_basis, in_basis, doc_lengths
):
    block_width = out_basis.shape[1]
    tok_count = layer_inputs.shape[0]
    tile_count = query_grads.shape[0]
    rows_out = query_grads.shape[2]
    rows_in = query_grads.shape[3]
    in_tiles = layer_inputs.shape[1] // rows_in
    out_tiles = output_grads.shape[1] // rows_out
    tile_ids = lax.axis_index("dp") * tile_count + lax.iota(jnp.int32, tile_count)
    out_sets = out_basis.reshape(out_tiles, rows_out // block_width, block_width, block_width)
    in_sets = in_basis.reshape(in_tiles, rows_in // block_width, block_width, block_width)
    tile_out = jnp.take(out_sets, tile_ids // in_tiles, axis=0)
    tile_in = jnp.take(in_sets, tile_ids % in_tiles, axis=0)
    eigen_sum = lax.psum(jnp.sum(eigenvalues), "dp")
    entries = output_grads.shape[1] * layer_inputs.shape[1]
    damping = 0.1 * (eigen_sum / entries)
    preconditioned = precondition(query_grads, eigenvalues, damping, tile_out, tile_in)
    grads_local = turn_rows(output_grads, out_basis)
    inputs_local = turn_rows(layer_inputs, in_basis)
    grads_tiles = grads_local.reshape(tok_count, out_tiles, rows_out).transpose(1, 0, 2)[:, None]
    grads_tiles = jnp.broadcast_to(grads_tiles, (out_tiles, in_tiles, tok_count, rows_out))
    grads_tiles = grads_tiles.reshape(out_tiles * in_tiles, tok_count, rows_out)
    inputs_tiles = inputs_local.reshape(tok_count, in_tiles, rows_in).transpose(1, 0, 2)[None]
    inputs_tiles = jnp.broadcast_to(inputs_tiles, (out_tiles, in_tiles, tok_count, rows_in))
    inputs_tiles = inputs_tiles.reshape(out_tiles * in_tiles, tok_count, rows_in)
    grads_got, inputs_got = (
        lax.all_to_all(grads_tiles, "dp", split_axis=0, concat_axis=1, tiled=True),
        lax.all_to_all(inputs_tiles, "dp", split_axis=0, concat_axis=1, tiled=True),
    )
    doc_ends = jnp.cumsum(doc_lengths)
    doc_starts = doc_ends - doc_lengths
    partial_scores = tally_scores(grads_got, inputs_got, preconditioned, doc_starts, doc_ends)
    return lax.psum_scatter(partial_scores, "dp", scatter_dimension=0, tiled=True)


def dot_nt(a, b):
    return lax.dot_general(a, b, (((1,), (1,)), ((), ())), preferred_element_type=F32)


def dot_tn(a, b):
    return lax.dot_general(a, b, (((0,), (0,)), ((), ())), preferred_element_type=F32)


def dot_tt(a, b):
    return lax.dot_general(a, b, (((0,), (1,)), ((), ())), preferred_element_type=F32)


def call(body, flops, bytes_accessed, **kw):
    return pl.pallas_call(
        body,
        compiler_params=pltpu.CompilerParams(vmem_limit_bytes=VMEM_LIMIT),
        cost_estimate=pl.CostEstimate(
            flops=flops, bytes_accessed=bytes_accessed, transcendentals=0
        ),
        **kw,
    )


def rotate_inputs(layer_inputs, in_basis):
    tokens, features = layer_inputs.shape
    count, width, _ = in_basis.shape

    def body(x_ref, b_ref, o_ref):
        for n in range(count):
            cols = slice(n * width, (n + 1) * width)
            o_ref[:, cols] = jnp.dot(
                x_ref[:, cols], b_ref[n], preferred_element_type=F32
            ).astype(BF16)

    return call(
        body,
        2 * tokens * features * width,
        4 * tokens * features + 2 * features * width,
        out_shape=jax.ShapeDtypeStruct((tokens, features), BF16),
        name="rotate_inputs",
    )(layer_inputs, in_basis)


def rotate_grads(output_grads, out_basis, chip, chips):
    tokens, units = output_grads.shape
    width = out_basis.shape[1]
    part = units // chips
    per = part // width

    def body(chip_ref, g_ref, b_ref, *o_refs):
        step = pl.program_id(0)
        for k in range(chips):

            @pl.when(step == k)
            def _():
                for n in range(per):
                    cols = slice(n * width, (n + 1) * width)
                    o_refs[k][cols, :] = dot_tt(b_ref[n], g_ref[:, cols]).astype(BF16)

    grid_spec = pltpu.PrefetchScalarGridSpec(
        num_scalar_prefetch=1,
        grid=(chips,),
        in_specs=[
            pl.BlockSpec((tokens, part), lambda k, c: (0, k ^ c[0])),
            pl.BlockSpec((per, width, width), lambda k, c: (k ^ c[0], 0, 0)),
        ],
        out_specs=[pl.BlockSpec((part, tokens), lambda k, c: (0, 0))] * chips,
    )
    return call(
        body,
        2 * tokens * units * width,
        4 * tokens * units + 2 * units * width,
        grid_spec=grid_spec,
        out_shape=[jax.ShapeDtypeStruct((part, tokens), BF16)] * chips,
        name="rotate_grads",
    )(chip[None], output_grads, out_basis)


def sum_eigenvalues(eigenvalues):
    tiles, rows, cols = eigenvalues.shape

    def body(e_ref, o_ref):
        @pl.when(pl.program_id(0) == 0)
        def _():
            o_ref[...] = jnp.zeros_like(o_ref)

        part = jnp.sum(e_ref[0].reshape(rows // 8, 8, cols), axis=0)
        total = part[:, :128]
        for n in range(1, cols // 128):
            total = total + part[:, n * 128 : (n + 1) * 128]
        o_ref[...] += total

    return call(
        body,
        tiles * rows * cols,
        4 * tiles * rows * cols,
        grid=(tiles,),
        in_specs=[pl.BlockSpec((1, rows, cols), lambda b: (b, 0, 0))],
        out_specs=pl.BlockSpec((8, 128), lambda b: (0, 0)),
        out_shape=jax.ShapeDtypeStruct((8, 128), F32),
        name="sum_eigenvalues",
    )(eigenvalues)


def precondition_rows(query_grads, eigenvalues, sums, out_basis, in_basis, me, entries):
    tiles, queries, rows, cols = query_grads.shape
    width = in_basis.shape[1]
    features = in_basis.shape[0] * width
    in_tiles = features // cols
    groups = tiles // in_tiles
    n_out, n_in = rows // width, cols // width

    def body(me_ref, q_ref, e_ref, s_ref, ob_ref, ib_ref, o_ref):
        damping = 0.1 * (jnp.sum(s_ref[...], keepdims=True) / entries)
        scale = 1.0 / (e_ref[0] + damping)
        for q in range(queries):
            half = [
                jnp.dot(
                    q_ref[0, q, :, n * width : (n + 1) * width],
                    ib_ref[n],
                    preferred_element_type=F32,
                ).astype(BF16)
                for n in range(n_in)
            ]
            half = jnp.concatenate(half, axis=1)
            for n in range(n_out):
                span = slice(n * width, (n + 1) * width)
                turned = dot_tn(ob_ref[n], half[span, :])
                o_ref[q, span, :] = (turned * scale[span, :]).astype(BF16)

    grid_spec = pltpu.PrefetchScalarGridSpec(
        num_scalar_prefetch=1,
        grid=(tiles,),
        in_specs=[
            pl.BlockSpec((1, queries, rows, cols), lambda b, m: (b, 0, 0, 0)),
            pl.BlockSpec((1, rows, cols), lambda b, m: (b, 0, 0)),
            pl.BlockSpec(sums.shape, lambda b, m: (0, 0)),
            pl.BlockSpec((n_out, width, width), lambda b, m: (m[0] * groups + b // in_tiles, 0, 0)),
            pl.BlockSpec((n_in, width, width), lambda b, m: (b % in_tiles, 0, 0)),
        ],
        out_specs=pl.BlockSpec(
            (queries, rows, cols), lambda b, m: (0, b // in_tiles, b % in_tiles)
        ),
    )
    return call(
        body,
        4 * tiles * queries * rows * cols * width,
        tiles * rows * cols * (4 + 4 * queries),
        grid_spec=grid_spec,
        out_shape=jax.ShapeDtypeStruct((queries, groups * rows, features), BF16),
        name="precondition",
    )(me[None], query_grads, eigenvalues, sums, out_basis, in_basis)


def tally(where, inputs, grads, own, sibling, starts, ends, running):
    pieces = len(inputs)
    tokens, features = inputs[0].shape
    part = grads[0].shape[0]
    queries, rows, _ = own.shape
    block = min(rows, 512)
    per = rows // block
    steps = queries * per
    docs = starts.shape[0]

    def body(where_ref, *refs):
        x_refs = refs[:pieces]
        g_refs = refs[pieces : 2 * pieces]
        own_ref, sib_ref, st_ref, en_ref, run_ref, o_ref, x_all = refs[2 * pieces :]
        step = pl.program_id(0)

        @pl.when(step == 0)
        def _():
            o_ref[...] = run_ref[...]
            for n in range(pieces):
                x_all[n * tokens : (n + 1) * tokens, :] = x_refs[n][...]

        def go(p_ref):
            query = lax.rem(step, steps) // per
            turned = dot_nt(p_ref[0], x_all[...])
            for n in range(pieces):
                score = jnp.sum(
                    turned[:, n * tokens : (n + 1) * tokens] * g_refs[n][...].astype(F32),
                    axis=0,
                    keepdims=True,
                )
                spot = where_ref[1 + n] * tokens + lax.broadcasted_iota(
                    jnp.int32, (docs, tokens), 1
                )
                inside = (spot >= st_ref[...]) & (spot < en_ref[...])
                o_ref[query] += jnp.where(inside, score, 0.0)

        @pl.when(step < steps)
        def _():
            go(own_ref)

        @pl.when(step >= steps)
        def _():
            go(sib_ref)

    def g_map(s, w):
        core = jnp.where(s < steps, w[0], 1 - w[0])
        return (core * per + lax.rem(s, per), 0)

    def own_map(s, w):
        s = jnp.minimum(s, steps - 1)
        return (s // per, lax.rem(s, per), 0)

    def sib_map(s, w):
        s = jnp.maximum(s - steps, 0)
        return (s // per, lax.rem(s, per), 0)

    whole = lambda a: pl.BlockSpec(a.shape, lambda s, w: (0,) * len(a.shape))
    grid_spec = pltpu.PrefetchScalarGridSpec(
        num_scalar_prefetch=1,
        grid=(2 * steps,),
        in_specs=[whole(x) for x in inputs]
        + [pl.BlockSpec((block, tokens), g_map) for _ in grads]
        + [
            pl.BlockSpec((1, block, features), own_map),
            pl.BlockSpec((1, block, features), sib_map),
            whole(starts),
            whole(ends),
            whole(running),
        ],
        out_specs=whole(running),
        scratch_shapes=[pltpu.VMEM((pieces * tokens, features), BF16)],
    )
    return call(
        body,
        4 * pieces * tokens * features * queries * rows,
        4 * queries * rows * features + pieces * tokens * 2 * (features + part),
        grid_spec=grid_spec,
        out_shape=jax.ShapeDtypeStruct(running.shape, F32),
        name="tally",
    )(where, *inputs, *grads, own, sibling, starts, ends, running)


def local_rows(
    depth, layer_inputs, output_grads, query_grads, eigenvalues, out_basis, in_basis, doc_lengths
):
    devices = 4 * depth
    chips = 2 * depth
    tokens = layer_inputs.shape[0]
    queries = query_grads.shape[1]
    entries = output_grads.shape[1] * layer_inputs.shape[1]
    me = lax.axis_index("dp")
    chip = me // 2
    core = me % 2

    def swap(value, offset):
        return lax.ppermute(value, "dp", [(i, i ^ offset) for i in range(devices)])

    x = rotate_inputs(layer_inputs, in_basis)
    sums = lax.all_gather(sum_eigenvalues(eigenvalues), "dp", tiled=True)
    g = rotate_grads(output_grads, out_basis, chip, chips)

    xs = [x] + [None] * (chips - 1)
    xs[6] = swap(x, 12)
    xs[2] = swap(x, 4)
    xs[1] = swap(x, 2)
    xs[4] = swap(xs[6], 4)
    xs[3] = swap(xs[2], 2)
    xs[7] = swap(xs[6], 2)
    xs[5] = swap(xs[4], 2)
    gs = [g[0]] + [swap(g[k], 2 * k) for k in range(1, chips)]

    own = precondition_rows(query_grads, eigenvalues, sums, out_basis, in_basis, me, entries)
    sibling = swap(own, 1)

    doc_ends = jnp.cumsum(doc_lengths)
    doc_starts = doc_ends - doc_lengths
    docs = doc_lengths.shape[0]
    starts = jnp.broadcast_to(doc_starts[:, None], (docs, tokens))
    ends = jnp.broadcast_to(doc_ends[:, None], (docs, tokens))
    running = jnp.zeros((queries, docs, tokens), F32)
    for pair in ((0, 1), (2, 3), (6, 7), (4, 5)):
        where = jnp.stack([core] + [me ^ (2 * k) for k in pair]).astype(jnp.int32)
        running = tally(
            where, [xs[k] for k in pair], [gs[k] for k in pair], own, sibling, starts, ends, running
        )
    shares = jnp.sum(running, axis=2)
    for offset in (1, 2, 4, 8):
        shares = shares + swap(shares, offset)
    each = docs // devices
    mine = lax.dynamic_slice_in_dim(shares, me * each, each, 1)
    return mine.T


def local(layer_inputs, output_grads, query_grads, eigenvalues, out_basis, in_basis, doc_lengths, devices):
    args = (layer_inputs, output_grads, query_grads, eigenvalues, out_basis, in_basis, doc_lengths)
    in_tiles = layer_inputs.shape[1] // query_grads.shape[3]
    tile_count = query_grads.shape[0]
    if devices == 16 and tile_count % in_tiles == 0:
        return local_rows(devices // 4, *args)
    return local_general(*args)


def solution(mesh):
    in_specs = (
        P(("groups", "dp"), None),
        P(("groups", "dp"), None),
        P("dp", None, None, None),
        P("dp", None, None),
        P(),
        P(),
        P("groups"),
    )
    out_specs = P(("groups", "dp"), None)
    body = functools.partial(local, devices=mesh.shape["dp"])
    return jax.shard_map(body, mesh=mesh, in_specs=in_specs, out_specs=out_specs, check_vma=False)
```

```python
import functools
import math

import jax
import jax.numpy as jnp
from jax import lax
from jax.experimental import pallas as pl
from jax.experimental.pallas import tpu as pltpu
from jax.sharding import PartitionSpec as P

VMEM_LIMIT = 16 * 1024 * 1024
COST_PRE = 10**11
COST_K3 = 10**11
F32 = jnp.float32
BF16 = jnp.bfloat16


def turn_rows(columns, basis_blocks):
    group_count = basis_blocks.shape[0]
    block_width = basis_blocks.shape[1]
    grouped = columns.reshape(columns.shape[0], group_count, block_width)
    turned = jnp.einsum("tnk,nkj->tnj", grouped, basis_blocks, preferred_element_type=jnp.float32)
    return turned.reshape(columns.shape).astype(jnp.bfloat16)


def precondition(query_grads, eigenvalues, damping, tile_out, tile_in):
    blocks, queries, rows_out, rows_in = query_grads.shape
    block_width = tile_in.shape[-1]
    grouped = query_grads.reshape(blocks, queries, rows_out, rows_in // block_width, block_width)
    half_turned = jnp.einsum(
        "bqonk,bnkj->bqonj", grouped, tile_in, preferred_element_type=jnp.float32
    )
    half_turned = half_turned.reshape(blocks, queries, rows_out, rows_in).astype(jnp.bfloat16)
    grouped = half_turned.reshape(blocks, queries, rows_out // block_width, block_width, rows_in)
    turned = jnp.einsum("bqnki,bnkj->bqnji", grouped, tile_out, preferred_element_type=jnp.float32)
    turned = turned.reshape(blocks, queries, rows_out, rows_in)
    return (turned / (eigenvalues[:, None] + damping)).astype(jnp.bfloat16)


def tally_scores(grads_got, inputs_got, preconditioned, doc_starts, doc_ends):
    blocks, total_rows, rows_out = grads_got.shape
    queries = preconditioned.shape[1]
    row_step = math.gcd(1024, total_rows)
    flat_pre = preconditioned.reshape(blocks, queries * rows_out, preconditioned.shape[3])

    def one_piece(running, piece_index):
        start_row = piece_index * row_step
        grads_piece = lax.dynamic_slice_in_dim(grads_got, start_row, row_step, 1)
        inputs_piece = lax.dynamic_slice_in_dim(inputs_got, start_row, row_step, 1)
        projected = jnp.einsum(
            "bti,bpi->btp", inputs_piece, flat_pre, preferred_element_type=jnp.float32
        )
        projected = projected.reshape(blocks, row_step, queries, rows_out)
        scores = jnp.sum(projected * grads_piece[:, :, None, :].astype(jnp.float32), axis=(0, 3))
        positions = start_row + lax.iota(jnp.int32, row_step)
        member = (
            (positions[:, None] >= doc_starts[None, :]) & (positions[:, None] < doc_ends[None, :])
        ).astype(jnp.float32)
        added = jnp.einsum("td,tq->dq", member, scores, precision=lax.Precision.HIGHEST)
        return (running + added, None)

    initial = jnp.zeros((doc_starts.shape[0], queries), jnp.float32)
    summed, _ = lax.scan(one_piece, initial, jnp.arange(total_rows // row_step, dtype=jnp.int32))
    return summed


def local_general(
    layer_inputs, output_grads, query_grads, eigenvalues, out_basis, in_basis, doc_lengths
):
    block_width = out_basis.shape[1]
    tok_count = layer_inputs.shape[0]
    tile_count = query_grads.shape[0]
    rows_out = query_grads.shape[2]
    rows_in = query_grads.shape[3]
    in_tiles = layer_inputs.shape[1] // rows_in
    out_tiles = output_grads.shape[1] // rows_out
    tile_ids = lax.axis_index("dp") * tile_count + lax.iota(jnp.int32, tile_count)
    out_sets = out_basis.reshape(out_tiles, rows_out // block_width, block_width, block_width)
    in_sets = in_basis.reshape(in_tiles, rows_in // block_width, block_width, block_width)
    tile_out = jnp.take(out_sets, tile_ids // in_tiles, axis=0)
    tile_in = jnp.take(in_sets, tile_ids % in_tiles, axis=0)
    eigen_sum = lax.psum(jnp.sum(eigenvalues), "dp")
    entries = output_grads.shape[1] * layer_inputs.shape[1]
    damping = 0.1 * (eigen_sum / entries)
    preconditioned = precondition(query_grads, eigenvalues, damping, tile_out, tile_in)
    grads_local = turn_rows(output_grads, out_basis)
    inputs_local = turn_rows(layer_inputs, in_basis)
    grads_tiles = grads_local.reshape(tok_count, out_tiles, rows_out).transpose(1, 0, 2)[:, None]
    grads_tiles = jnp.broadcast_to(grads_tiles, (out_tiles, in_tiles, tok_count, rows_out))
    grads_tiles = grads_tiles.reshape(out_tiles * in_tiles, tok_count, rows_out)
    inputs_tiles = inputs_local.reshape(tok_count, in_tiles, rows_in).transpose(1, 0, 2)[None]
    inputs_tiles = jnp.broadcast_to(inputs_tiles, (out_tiles, in_tiles, tok_count, rows_in))
    inputs_tiles = inputs_tiles.reshape(out_tiles * in_tiles, tok_count, rows_in)
    grads_got, inputs_got = (
        lax.all_to_all(grads_tiles, "dp", split_axis=0, concat_axis=1, tiled=True),
        lax.all_to_all(inputs_tiles, "dp", split_axis=0, concat_axis=1, tiled=True),
    )
    doc_ends = jnp.cumsum(doc_lengths)
    doc_starts = doc_ends - doc_lengths
    partial_scores = tally_scores(grads_got, inputs_got, preconditioned, doc_starts, doc_ends)
    return lax.psum_scatter(partial_scores, "dp", scatter_dimension=0, tiled=True)


def dot_tt(a, b):
    return lax.dot_general(a, b, (((0,), (1,)), ((), ())), preferred_element_type=F32)


def call(body, cost=1, **kw):
    return pl.pallas_call(
        body,
        compiler_params=pltpu.CompilerParams(vmem_limit_bytes=VMEM_LIMIT),
        cost_estimate=pl.CostEstimate(flops=cost, bytes_accessed=1, transcendentals=0),
        **kw,
    )


def in_hbm(value):
    return pltpu.with_memory_space_constraint(value, pltpu.HBM)


def rotate_inputs(layer_inputs, in_basis):
    tokens, features = layer_inputs.shape
    count, width, _ = in_basis.shape

    def body(x_hbm, b_hbm, o_ref, x_all, b_all, sems):
        copies = [
            pltpu.make_async_copy(x_hbm, x_all, sems.at[0]),
            pltpu.make_async_copy(b_hbm, b_all, sems.at[1]),
        ]
        for copy in copies:
            copy.start()
        for copy in copies:
            copy.wait()
        for n in range(count):
            span = slice(n * width, (n + 1) * width)
            turned = jnp.dot(x_all[:, span], b_all[n], preferred_element_type=F32)
            o_ref[span, :] = turned.astype(BF16).T

    hbm = pl.BlockSpec(memory_space=pl.ANY)
    return call(
        body,
        in_specs=[hbm, hbm],
        out_specs=pl.BlockSpec(memory_space=pltpu.VMEM),
        out_shape=jax.ShapeDtypeStruct((features, tokens), BF16),
        scratch_shapes=[
            pltpu.VMEM((tokens, features), BF16),
            pltpu.VMEM((count, width, width), BF16),
            pltpu.SemaphoreType.DMA((2,)),
        ],
        name="rotate_inputs",
    )(in_hbm(layer_inputs), in_hbm(in_basis))


def rotate_grads(output_grads, out_basis, chip, chips, layouts, sources=(), after=(), cost=1):
    tokens, units = output_grads.shape
    width = out_basis.shape[1]
    part = units // chips
    per = part // width
    offsets = [k for layout in layouts for k in layout if isinstance(k, int)]
    count = len(offsets)
    heights = [sum(part if isinstance(k, int) else k[2] for k in layout) for layout in layouts]
    extra = list(sources) + list(after)

    def body(chip_ref, g_hbm, b_hbm, *refs):
        o_refs = refs[len(extra) : len(extra) + len(layouts)]
        g_all, b_all, g_sems, b_sems = refs[len(extra) + len(layouts) :]
        copies = []
        for n, k in enumerate(offsets):
            place = chip_ref[0] ^ k
            cols = pl.ds(pl.multiple_of(place * part, part), part)
            blocks = pl.ds(place * per, per)
            copies.append(
                (
                    pltpu.make_async_copy(g_hbm.at[:, cols], g_all.at[n], g_sems.at[n]),
                    pltpu.make_async_copy(b_hbm.at[blocks], b_all.at[n], b_sems.at[n]),
                )
            )
        for pair in copies:
            for copy in pair:
                copy.start()
        n = 0
        for o_ref, layout in zip(o_refs, layouts):
            top = 0
            for k in layout:
                if not isinstance(k, int):
                    source, first, rows = k
                    o_ref[top : top + rows, :] = refs[source][first : first + rows, :]
                    top += rows
                    continue
                for copy in copies[n]:
                    copy.wait()
                for i in range(per):
                    span = slice(i * width, (i + 1) * width)
                    turned = jnp.dot(g_all[n, :, span], b_all[n, i], preferred_element_type=F32)
                    o_ref[top + i * width : top + (i + 1) * width, :] = turned.astype(BF16).T
                top += part
                n += 1

    hbm = pl.BlockSpec(memory_space=pl.ANY)
    vmem = pl.BlockSpec(memory_space=pltpu.VMEM)
    return call(
        body,
        in_specs=[pl.BlockSpec(memory_space=pltpu.SMEM), hbm, hbm]
        + [vmem] * len(sources)
        + [hbm] * len(after),
        out_specs=[vmem] * len(layouts),
        out_shape=[jax.ShapeDtypeStruct((h, tokens), BF16) for h in heights],
        scratch_shapes=[
            pltpu.VMEM((count, tokens, part), BF16),
            pltpu.VMEM((count, per, width, width), BF16),
            pltpu.SemaphoreType.DMA((count,)),
            pltpu.SemaphoreType.DMA((count,)),
        ],
        name="rotate_grads",
        cost=cost,
    )(chip[None], output_grads, out_basis, *extra)


def sum_eigenvalues(eigenvalues):
    tiles, rows, cols = eigenvalues.shape

    def body(e_ref, o_ref):
        @pl.when(pl.program_id(0) == 0)
        def _():
            o_ref[...] = jnp.zeros_like(o_ref)

        part = jnp.sum(e_ref[0].reshape(rows // 8, 8, cols), axis=0)
        total = part[:, :128]
        for n in range(1, cols // 128):
            total = total + part[:, n * 128 : (n + 1) * 128]
        o_ref[...] += total

    return call(
        body,
        grid=(tiles,),
        in_specs=[pl.BlockSpec((1, rows, cols), lambda b: (b, 0, 0))],
        out_specs=pl.BlockSpec((8, 128), lambda b: (0, 0)),
        out_shape=jax.ShapeDtypeStruct((8, 128), F32),
        name="sum_eigenvalues",
    )(eigenvalues)


def add_after(a, b, *after):
    def body(a_ref, b_ref, *refs):
        refs[-1][...] = a_ref[...] + b_ref[...]

    vmem = pl.BlockSpec(memory_space=pltpu.VMEM)
    return call(
        body,
        in_specs=[vmem, vmem] + [pl.BlockSpec(memory_space=pl.ANY)] * len(after),
        out_specs=vmem,
        out_shape=jax.ShapeDtypeStruct(a.shape, a.dtype),
        name="add_after",
    )(a, b, *after)


def block_diagonal(blocks):
    count, width = len(blocks), blocks[0].shape[0]
    zero = jnp.zeros((width, width), blocks[0].dtype)
    rows = [
        jnp.concatenate([blocks[i] if i == j else zero for j in range(count)], axis=1)
        for i in range(count)
    ]
    return jnp.concatenate(rows, axis=0)


def precondition_rows(query_grads, eigenvalues, sums, out_basis, in_basis, me, entries, after):
    tiles, queries, rows, cols = query_grads.shape
    width = in_basis.shape[1]
    features = in_basis.shape[0] * width
    in_tiles = features // cols
    groups = tiles // in_tiles
    n_out, n_in = rows // width, cols // width
    pair = 2 if n_out % 2 == 0 else 1
    span = pair * width

    def body(me_ref, q_ref, e_ref, s_ref, ob_ref, ib_ref, *refs):
        o_ref, turn_ref = refs[len(after) :]

        @pl.when(pl.program_id(0) % in_tiles == 0)
        def _():
            for n in range(n_out // pair):
                turn_ref[n] = block_diagonal([ob_ref[n * pair + k].T for k in range(pair)])

        damping = 0.1 * (jnp.sum(s_ref[...], keepdims=True) / entries)
        scale = 1.0 / (e_ref[0] + damping)
        half = jnp.dot(
            q_ref[0].reshape(queries * rows, cols),
            block_diagonal([ib_ref[n] for n in range(n_in)]),
            preferred_element_type=F32,
        ).astype(BF16)
        for q in range(queries):
            for n in range(n_out // pair):
                start = n * span
                turned = jnp.dot(
                    turn_ref[n],
                    half[q * rows + start : q * rows + start + span],
                    preferred_element_type=F32,
                )
                o_ref[q, start : start + span, :] = (turned * scale[start : start + span]).astype(
                    BF16
                )

    grid_spec = pltpu.PrefetchScalarGridSpec(
        num_scalar_prefetch=1,
        grid=(tiles,),
        in_specs=[
            pl.BlockSpec((1, queries, rows, cols), lambda b, m: (b, 0, 0, 0)),
            pl.BlockSpec((1, rows, cols), lambda b, m: (b, 0, 0)),
            pl.BlockSpec(sums.shape, lambda b, m: (0, 0)),
            pl.BlockSpec((n_out, width, width), lambda b, m: (m[0] * groups + b // in_tiles, 0, 0)),
            pl.BlockSpec((n_in, width, width), lambda b, m: (b % in_tiles, 0, 0)),
        ]
        + [pl.BlockSpec(memory_space=pl.ANY)] * len(after),
        out_specs=pl.BlockSpec(
            (queries, rows, cols), lambda b, m: (0, b // in_tiles, b % in_tiles)
        ),
        scratch_shapes=[pltpu.VMEM((n_out // pair, span, span), BF16)],
    )
    return call(
        body,
        grid_spec=grid_spec,
        out_shape=jax.ShapeDtypeStruct((queries, groups * rows, features), BF16),
        name="precondition",
        cost=COST_PRE,
    )(me[None], query_grads, eigenvalues, sums, out_basis, in_basis, *after)


def join_rows(own, sibling, core, after):
    def body(core_ref, own_ref, sib_ref, *refs):
        o_ref, sems = refs[len(after) :]
        copies = [
            pltpu.make_async_copy(own_ref, o_ref.at[core_ref[0]], sems.at[0]),
            pltpu.make_async_copy(sib_ref, o_ref.at[1 - core_ref[0]], sems.at[1]),
        ]
        for copy in copies:
            copy.start()
        for copy in copies:
            copy.wait()

    hbm = pl.BlockSpec(memory_space=pl.ANY)
    return call(
        body,
        in_specs=[pl.BlockSpec(memory_space=pltpu.SMEM), hbm, hbm] + [hbm] * len(after),
        out_specs=pl.BlockSpec(memory_space=pltpu.VMEM),
        out_shape=jax.ShapeDtypeStruct((2,) + own.shape, own.dtype),
        scratch_shapes=[pltpu.SemaphoreType.DMA((2,))],
        name="join_rows",
    )(core[None], own, sibling, *after)


def tally(where, pieces, both, starts, ends, running):
    count = len(pieces)
    cores, queries, rows, features = both.shape
    tokens = starts.shape[1]
    block = math.gcd(rows, 512)
    docs = starts.shape[0]
    arrays = []
    places = []
    for piece in pieces:
        for array, _ in piece:
            if not any(array is other for other in arrays):
                arrays.append(array)
        places.append([next(i for i, o in enumerate(arrays) if o is a) for a, _ in piece])

    def body(where_ref, *refs):
        p_ref, st_ref, en_ref, run_ref, o_ref, x_all = refs[len(arrays) :]
        for n in range(count):
            first = pieces[n][0][1]
            x_all[:, n * tokens : (n + 1) * tokens] = refs[places[n][0]][first : first + features, :]
        scores = [[jnp.zeros((1, tokens), F32)] * queries for _ in range(count)]
        for c in range(cores):
            for q in range(queries):
                for r in range(0, rows, block):
                    turned = jnp.dot(
                        p_ref[c, q, r : r + block, :], x_all[...], preferred_element_type=F32
                    )
                    for n in range(count):
                        first = pieces[n][1][1] + c * rows + r
                        scores[n][q] = scores[n][q] + jnp.sum(
                            turned[:, n * tokens : (n + 1) * tokens]
                            * refs[places[n][1]][first : first + block, :].astype(F32),
                            axis=0,
                            keepdims=True,
                        )
        for q in range(queries):
            total = run_ref[q]
            for n in range(count):
                spot = where_ref[n] * tokens + lax.broadcasted_iota(jnp.int32, (docs, tokens), 1)
                inside = (spot >= st_ref[...]) & (spot < en_ref[...])
                total = total + jnp.where(inside, scores[n][q], 0.0)
            o_ref[q] = total

    vmem = pl.BlockSpec(memory_space=pltpu.VMEM)
    return call(
        body,
        in_specs=[pl.BlockSpec(memory_space=pltpu.SMEM)] + [vmem] * (len(arrays) + 4),
        out_specs=vmem,
        out_shape=jax.ShapeDtypeStruct(running.shape, F32),
        scratch_shapes=[pltpu.VMEM((features, count * tokens), BF16)],
        name="tally",
    )(where, *arrays, both, starts, ends, running)


def local_rows(
    depth, layer_inputs, output_grads, query_grads, eigenvalues, out_basis, in_basis, doc_lengths
):
    devices = 4 * depth
    chips = 2 * depth
    tokens = layer_inputs.shape[0]
    queries = query_grads.shape[1]
    entries = output_grads.shape[1] * layer_inputs.shape[1]
    me = lax.axis_index("dp")
    chip = me // 2
    core = me % 2

    def swap(value, offset):
        return lax.ppermute(value, "dp", [(i, i ^ offset) for i in range(devices)])

    features = layer_inputs.shape[1]
    part = output_grads.shape[1] // chips
    x = rotate_inputs(layer_inputs, in_basis)
    rotate = functools.partial(rotate_grads, in_hbm(output_grads), in_hbm(out_basis), chip, chips)
    side, near_side_g, g_own = rotate([[(0, 0, features), 1], [3], [0]], [x])
    far_x = swap(x, 12)
    near_x = swap(x, 4)
    side = swap(side, 2)
    near_side_g = swap(near_side_g, 6)
    first = [far_x, near_x, side, near_side_g]

    sums = sum_eigenvalues(eigenvalues)
    for offset in (1, 2, 4, 8):
        sums = sums + swap(sums, offset)

    (middle,) = rotate([[4, 5]], [], first)
    middle = swap(middle, 8)
    middle_x = swap(far_x, 4)
    near_x_side = swap(near_x, 2)
    far_x_side = swap(far_x, 2)
    second = [middle, middle_x, near_x_side, far_x_side]

    own = precondition_rows(
        query_grads, eigenvalues, sums, out_basis, in_basis, me, entries, first
    )
    both = join_rows(own, swap(own, 1), core, second)

    middle_side, g_far, g_far_side, near_g = rotate(
        [[(0, 0, features), (1, part, part)], [6], [7], [2]],
        [middle_x, middle],
        second + [own],
        cost=COST_K3,
    )
    middle_side = swap(middle_side, 2)
    g_far = swap(g_far, 12)
    g_far_side = swap(g_far_side, 14)
    near_g = swap(near_g, 4)

    doc_ends = jnp.cumsum(doc_lengths)
    doc_starts = doc_ends - doc_lengths
    docs = doc_lengths.shape[0]
    starts = jnp.broadcast_to(doc_starts[:, None], (docs, tokens))
    ends = jnp.broadcast_to(doc_ends[:, None], (docs, tokens))
    running = jnp.zeros((queries, docs, tokens), F32)
    pieces = {
        0: ((x, 0), (g_own, 0)),
        1: ((side, 0), (side, features)),
        2: ((near_x, 0), (near_g, 0)),
        3: ((near_x_side, 0), (near_side_g, 0)),
        4: ((middle_x, 0), (middle, 0)),
        5: ((middle_side, 0), (middle_side, features)),
        6: ((far_x, 0), (g_far, 0)),
        7: ((far_x_side, 0), (g_far_side, 0)),
    }
    for some in ((0, 1, 3, 4), (2, 6), (5, 7)):
        where = jnp.stack([me ^ (2 * k) for k in some]).astype(jnp.int32)
        running = tally(where, [pieces[k] for k in some], both, starts, ends, running)
    shares = jnp.sum(running, axis=2)
    for offset in (1, 2, 4, 8):
        shares = shares + swap(shares, offset)
    each = docs // devices
    mine = lax.dynamic_slice_in_dim(shares, me * each, each, 1)
    return mine.T


def local(layer_inputs, output_grads, query_grads, eigenvalues, out_basis, in_basis, doc_lengths, devices):
    args = (layer_inputs, output_grads, query_grads, eigenvalues, out_basis, in_basis, doc_lengths)
    in_tiles = layer_inputs.shape[1] // query_grads.shape[3]
    tile_count = query_grads.shape[0]
    if devices == 16 and tile_count % in_tiles == 0:
        return local_rows(devices // 4, *args)
    return local_general(*args)


def solution(mesh):
    in_specs = (
        P(("groups", "dp"), None),
        P(("groups", "dp"), None),
        P("dp", None, None, None),
        P("dp", None, None),
        P(),
        P(),
        P("groups"),
    )
    out_specs = P(("groups", "dp"), None)
    body = functools.partial(local, devices=mesh.shape["dp"])
    return jax.shard_map(body, mesh=mesh, in_specs=in_specs, out_specs=out_specs, check_vma=False)
```

```python
import functools
import math

import jax
import jax.numpy as jnp
from jax import lax
from jax.experimental import pallas as pl
from jax.experimental.pallas import tpu as pltpu
from jax.sharding import PartitionSpec as P

VMEM_LIMIT = 16 * 1024 * 1024
COST_PRE = 10**11
COST_K3 = 10**11
F32 = jnp.float32
BF16 = jnp.bfloat16


def turn_rows(columns, basis_blocks):
    group_count = basis_blocks.shape[0]
    block_width = basis_blocks.shape[1]
    grouped = columns.reshape(columns.shape[0], group_count, block_width)
    turned = jnp.einsum("tnk,nkj->tnj", grouped, basis_blocks, preferred_element_type=jnp.float32)
    return turned.reshape(columns.shape).astype(jnp.bfloat16)


def precondition(query_grads, eigenvalues, damping, tile_out, tile_in):
    blocks, queries, rows_out, rows_in = query_grads.shape
    block_width = tile_in.shape[-1]
    grouped = query_grads.reshape(blocks, queries, rows_out, rows_in // block_width, block_width)
    half_turned = jnp.einsum(
        "bqonk,bnkj->bqonj", grouped, tile_in, preferred_element_type=jnp.float32
    )
    half_turned = half_turned.reshape(blocks, queries, rows_out, rows_in).astype(jnp.bfloat16)
    grouped = half_turned.reshape(blocks, queries, rows_out // block_width, block_width, rows_in)
    turned = jnp.einsum("bqnki,bnkj->bqnji", grouped, tile_out, preferred_element_type=jnp.float32)
    turned = turned.reshape(blocks, queries, rows_out, rows_in)
    return (turned / (eigenvalues[:, None] + damping)).astype(jnp.bfloat16)


def tally_scores(grads_got, inputs_got, preconditioned, doc_starts, doc_ends):
    blocks, total_rows, rows_out = grads_got.shape
    queries = preconditioned.shape[1]
    row_step = math.gcd(1024, total_rows)
    flat_pre = preconditioned.reshape(blocks, queries * rows_out, preconditioned.shape[3])

    def one_piece(running, piece_index):
        start_row = piece_index * row_step
        grads_piece = lax.dynamic_slice_in_dim(grads_got, start_row, row_step, 1)
        inputs_piece = lax.dynamic_slice_in_dim(inputs_got, start_row, row_step, 1)
        projected = jnp.einsum(
            "bti,bpi->btp", inputs_piece, flat_pre, preferred_element_type=jnp.float32
        )
        projected = projected.reshape(blocks, row_step, queries, rows_out)
        scores = jnp.sum(projected * grads_piece[:, :, None, :].astype(jnp.float32), axis=(0, 3))
        positions = start_row + lax.iota(jnp.int32, row_step)
        member = (
            (positions[:, None] >= doc_starts[None, :]) & (positions[:, None] < doc_ends[None, :])
        ).astype(jnp.float32)
        added = jnp.einsum("td,tq->dq", member, scores, precision=lax.Precision.HIGHEST)
        return (running + added, None)

    initial = jnp.zeros((doc_starts.shape[0], queries), jnp.float32)
    summed, _ = lax.scan(one_piece, initial, jnp.arange(total_rows // row_step, dtype=jnp.int32))
    return summed


def local_general(
    layer_inputs, output_grads, query_grads, eigenvalues, out_basis, in_basis, doc_lengths
):
    block_width = out_basis.shape[1]
    tok_count = layer_inputs.shape[0]
    tile_count = query_grads.shape[0]
    rows_out = query_grads.shape[2]
    rows_in = query_grads.shape[3]
    in_tiles = layer_inputs.shape[1] // rows_in
    out_tiles = output_grads.shape[1] // rows_out
    tile_ids = lax.axis_index("dp") * tile_count + lax.iota(jnp.int32, tile_count)
    out_sets = out_basis.reshape(out_tiles, rows_out // block_width, block_width, block_width)
    in_sets = in_basis.reshape(in_tiles, rows_in // block_width, block_width, block_width)
    tile_out = jnp.take(out_sets, tile_ids // in_tiles, axis=0)
    tile_in = jnp.take(in_sets, tile_ids % in_tiles, axis=0)
    eigen_sum = lax.psum(jnp.sum(eigenvalues), "dp")
    entries = output_grads.shape[1] * layer_inputs.shape[1]
    damping = 0.1 * (eigen_sum / entries)
    preconditioned = precondition(query_grads, eigenvalues, damping, tile_out, tile_in)
    grads_local = turn_rows(output_grads, out_basis)
    inputs_local = turn_rows(layer_inputs, in_basis)
    grads_tiles = grads_local.reshape(tok_count, out_tiles, rows_out).transpose(1, 0, 2)[:, None]
    grads_tiles = jnp.broadcast_to(grads_tiles, (out_tiles, in_tiles, tok_count, rows_out))
    grads_tiles = grads_tiles.reshape(out_tiles * in_tiles, tok_count, rows_out)
    inputs_tiles = inputs_local.reshape(tok_count, in_tiles, rows_in).transpose(1, 0, 2)[None]
    inputs_tiles = jnp.broadcast_to(inputs_tiles, (out_tiles, in_tiles, tok_count, rows_in))
    inputs_tiles = inputs_tiles.reshape(out_tiles * in_tiles, tok_count, rows_in)
    grads_got, inputs_got = (
        lax.all_to_all(grads_tiles, "dp", split_axis=0, concat_axis=1, tiled=True),
        lax.all_to_all(inputs_tiles, "dp", split_axis=0, concat_axis=1, tiled=True),
    )
    doc_ends = jnp.cumsum(doc_lengths)
    doc_starts = doc_ends - doc_lengths
    partial_scores = tally_scores(grads_got, inputs_got, preconditioned, doc_starts, doc_ends)
    return lax.psum_scatter(partial_scores, "dp", scatter_dimension=0, tiled=True)


def dot_tt(a, b):
    return lax.dot_general(a, b, (((0,), (1,)), ((), ())), preferred_element_type=F32)


def call(body, cost=1, **kw):
    return pl.pallas_call(
        body,
        compiler_params=pltpu.CompilerParams(vmem_limit_bytes=VMEM_LIMIT),
        cost_estimate=pl.CostEstimate(flops=cost, bytes_accessed=1, transcendentals=0),
        **kw,
    )


def in_hbm(value):
    return pltpu.with_memory_space_constraint(value, pltpu.HBM)


def rotate(output_grads, out_basis, chip, chips, layouts, layer_inputs=None, in_basis=None):
    tokens, units = output_grads.shape
    width = out_basis.shape[1]
    part = units // chips
    per = part // width
    offsets = [k for layout in layouts for k in layout if k is not None]
    count = len(offsets)
    features = 0 if layer_inputs is None else layer_inputs.shape[1]
    heights = [sum(features if k is None else part for k in layout) for layout in layouts]
    operands = [output_grads, out_basis]
    if features:
        operands += [layer_inputs, in_basis]

    def body(chip_ref, *refs):
        hbm_refs = refs[: len(operands)]
        o_refs = refs[len(operands) : len(operands) + len(layouts)]
        scratch = refs[len(operands) + len(layouts) :]
        g_all, b_all, g_sems, b_sems = scratch[:4]
        copies = []
        if features:
            x_all, xb_all, x_sems = scratch[4:]
            x_copies = [
                pltpu.make_async_copy(hbm_refs[2], x_all, x_sems.at[0]),
                pltpu.make_async_copy(hbm_refs[3], xb_all, x_sems.at[1]),
            ]
            for copy in x_copies:
                copy.start()
        for n, k in enumerate(offsets):
            place = chip_ref[0] ^ k
            cols = pl.ds(pl.multiple_of(place * part, part), part)
            blocks = pl.ds(place * per, per)
            copies.append(
                (
                    pltpu.make_async_copy(hbm_refs[0].at[:, cols], g_all.at[n], g_sems.at[n]),
                    pltpu.make_async_copy(hbm_refs[1].at[blocks], b_all.at[n], b_sems.at[n]),
                )
            )
        for pair in copies:
            for copy in pair:
                copy.start()
        if features:
            for copy in x_copies:
                copy.wait()
            for i in range(features // width):
                span = slice(i * width, (i + 1) * width)
                turned = jnp.dot(x_all[:, span], xb_all[i], preferred_element_type=F32)
                turned = turned.astype(BF16).T
                for o_ref, layout in zip(o_refs, layouts):
                    if None in layout:
                        top = part * layout.index(None)
                        o_ref[top + i * width : top + (i + 1) * width, :] = turned
        n = 0
        for o_ref, layout in zip(o_refs, layouts):
            top = 0
            for k in layout:
                if k is None:
                    top += features
                    continue
                for copy in copies[n]:
                    copy.wait()
                for i in range(per):
                    span = slice(i * width, (i + 1) * width)
                    turned = jnp.dot(g_all[n, :, span], b_all[n, i], preferred_element_type=F32)
                    o_ref[top + i * width : top + (i + 1) * width, :] = turned.astype(BF16).T
                top += part
                n += 1

    hbm = pl.BlockSpec(memory_space=pl.ANY)
    vmem = pl.BlockSpec(memory_space=pltpu.VMEM)
    scratch_shapes = [
        pltpu.VMEM((count, tokens, part), BF16),
        pltpu.VMEM((count, per, width, width), BF16),
        pltpu.SemaphoreType.DMA((count,)),
        pltpu.SemaphoreType.DMA((count,)),
    ]
    if features:
        scratch_shapes += [
            pltpu.VMEM((tokens, features), BF16),
            pltpu.VMEM(in_basis.shape, BF16),
            pltpu.SemaphoreType.DMA((2,)),
        ]
    return call(
        body,
        in_specs=[pl.BlockSpec(memory_space=pltpu.SMEM)] + [hbm] * len(operands),
        out_specs=[vmem] * len(layouts),
        out_shape=[jax.ShapeDtypeStruct((h, tokens), BF16) for h in heights],
        scratch_shapes=scratch_shapes,
        name="rotate",
    )(chip[None], *[in_hbm(value) for value in operands])


def pack(layouts, held, after, cost=1):
    arrays = []
    places = []
    for layout in layouts:
        for array, _, _ in layout:
            if not any(array is other for other in arrays):
                arrays.append(array)
        places.append([next(i for i, o in enumerate(arrays) if o is a) for a, _, _ in layout])
    operands = arrays + list(held) + list(after)

    def body(*refs):
        o_refs = refs[len(operands) : len(operands) + len(layouts)]
        for o_ref, layout, place in zip(o_refs, layouts, places):
            top = 0
            for (_, first, rows), i in zip(layout, place):
                o_ref[top : top + rows, :] = refs[i][first : first + rows, :]
                top += rows

    anywhere = pl.BlockSpec(memory_space=pl.ANY)
    vmem = pl.BlockSpec(memory_space=pltpu.VMEM)
    shapes = [
        jax.ShapeDtypeStruct((sum(rows for _, _, rows in layout), layout[0][0].shape[1]), BF16)
        for layout in layouts
    ]
    return call(
        body,
        cost=cost,
        in_specs=[vmem] * len(arrays) + [anywhere] * (len(held) + len(after)),
        out_specs=[vmem] * len(layouts) + [anywhere] * len(held),
        out_shape=shapes + [jax.ShapeDtypeStruct(h.shape, h.dtype) for h in held],
        input_output_aliases={len(arrays) + n: len(layouts) + n for n in range(len(held))},
        name="pack",
    )(*operands)


def sum_eigenvalues(eigenvalues):
    tiles, rows, cols = eigenvalues.shape

    def body(e_ref, o_ref):
        @pl.when(pl.program_id(0) == 0)
        def _():
            o_ref[...] = jnp.zeros_like(o_ref)

        part = jnp.sum(e_ref[0].reshape(rows // 8, 8, cols), axis=0)
        total = part[:, :128]
        for n in range(1, cols // 128):
            total = total + part[:, n * 128 : (n + 1) * 128]
        o_ref[...] += total

    return call(
        body,
        grid=(tiles,),
        in_specs=[pl.BlockSpec((1, rows, cols), lambda b: (b, 0, 0))],
        out_specs=pl.BlockSpec((8, 128), lambda b: (0, 0)),
        out_shape=jax.ShapeDtypeStruct((8, 128), F32),
        name="sum_eigenvalues",
    )(eigenvalues)


def hold(value, *after):
    def body(v_ref, *refs):
        refs[-1][...] = v_ref[...]

    vmem = pl.BlockSpec(memory_space=pltpu.VMEM)
    return call(
        body,
        in_specs=[vmem] + [pl.BlockSpec(memory_space=pl.ANY)] * len(after),
        out_specs=vmem,
        out_shape=jax.ShapeDtypeStruct(value.shape, value.dtype),
        name="hold",
    )(value, *after)


def block_diagonal(blocks):
    count, width = len(blocks), blocks[0].shape[0]
    zero = jnp.zeros((width, width), blocks[0].dtype)
    rows = [
        jnp.concatenate([blocks[i] if i == j else zero for j in range(count)], axis=1)
        for i in range(count)
    ]
    return jnp.concatenate(rows, axis=0)


def precondition_rows(query_grads, eigenvalues, sums, out_basis, in_basis, me, entries, after):
    tiles, queries, rows, cols = query_grads.shape
    width = in_basis.shape[1]
    features = in_basis.shape[0] * width
    in_tiles = features // cols
    groups = tiles // in_tiles
    n_out, n_in = rows // width, cols // width
    pair = 2 if n_out % 2 == 0 else 1
    span = pair * width

    def body(me_ref, q_ref, e_ref, s_ref, ob_ref, ib_ref, *refs):
        o_ref, turn_ref = refs[len(after) :]

        @pl.when(pl.program_id(0) % in_tiles == 0)
        def _():
            for n in range(n_out // pair):
                turn_ref[n] = block_diagonal([ob_ref[n * pair + k].T for k in range(pair)])

        damping = 0.1 * (jnp.sum(s_ref[...], keepdims=True) / entries)
        scale = 1.0 / (e_ref[0] + damping)
        half = jnp.dot(
            q_ref[0].reshape(queries * rows, cols),
            block_diagonal([ib_ref[n] for n in range(n_in)]),
            preferred_element_type=F32,
        ).astype(BF16)
        for q in range(queries):
            for n in range(n_out // pair):
                start = n * span
                turned = jnp.dot(
                    turn_ref[n],
                    half[q * rows + start : q * rows + start + span],
                    preferred_element_type=F32,
                )
                o_ref[q, start : start + span, :] = (turned * scale[start : start + span]).astype(
                    BF16
                )

    grid_spec = pltpu.PrefetchScalarGridSpec(
        num_scalar_prefetch=1,
        grid=(tiles,),
        in_specs=[
            pl.BlockSpec((1, queries, rows, cols), lambda b, m: (b, 0, 0, 0)),
            pl.BlockSpec((1, rows, cols), lambda b, m: (b, 0, 0)),
            pl.BlockSpec(sums.shape, lambda b, m: (0, 0)),
            pl.BlockSpec((n_out, width, width), lambda b, m: (m[0] * groups + b // in_tiles, 0, 0)),
            pl.BlockSpec((n_in, width, width), lambda b, m: (b % in_tiles, 0, 0)),
        ]
        + [pl.BlockSpec(memory_space=pl.ANY)] * len(after),
        out_specs=pl.BlockSpec(
            (queries, rows, cols), lambda b, m: (0, b // in_tiles, b % in_tiles)
        ),
        scratch_shapes=[pltpu.VMEM((n_out // pair, span, span), BF16)],
    )
    return call(
        body,
        grid_spec=grid_spec,
        out_shape=jax.ShapeDtypeStruct((queries, groups * rows, features), BF16),
        name="precondition",
        cost=COST_PRE,
    )(me[None], query_grads, eigenvalues, sums, out_basis, in_basis, *after)


def join_rows(own, sibling, core, after):
    def body(core_ref, own_ref, sib_ref, *refs):
        o_ref, sems = refs[len(after) :]
        copies = [
            pltpu.make_async_copy(own_ref, o_ref.at[core_ref[0]], sems.at[0]),
            pltpu.make_async_copy(sib_ref, o_ref.at[1 - core_ref[0]], sems.at[1]),
        ]
        for copy in copies:
            copy.start()
        for copy in copies:
            copy.wait()

    hbm = pl.BlockSpec(memory_space=pl.ANY)
    return call(
        body,
        in_specs=[pl.BlockSpec(memory_space=pltpu.SMEM), hbm, hbm] + [hbm] * len(after),
        out_specs=pl.BlockSpec(memory_space=pltpu.VMEM),
        out_shape=jax.ShapeDtypeStruct((2,) + own.shape, own.dtype),
        scratch_shapes=[pltpu.SemaphoreType.DMA((2,))],
        name="join_rows",
    )(core[None], own, sibling, *after)


def project(inputs, both, tokens, after):
    cores, queries, rows, features = both.shape
    block = math.gcd(rows, 512)

    def body(*refs):
        p_ref = refs[len(inputs)]
        for c in range(cores):
            for q in range(queries):
                for r in range(0, rows, block):
                    for n, (_, first) in enumerate(inputs):
                        refs[len(inputs) + 1 + len(after) + n][c, q, r : r + block, :] = jnp.dot(
                            p_ref[c, q, r : r + block, :],
                            refs[n][first : first + features, :],
                            preferred_element_type=F32,
                        )

    vmem = pl.BlockSpec(memory_space=pltpu.VMEM)
    return call(
        body,
        in_specs=[vmem] * (len(inputs) + 1) + [pl.BlockSpec(memory_space=pl.ANY)] * len(after),
        out_specs=[vmem] * len(inputs),
        out_shape=[jax.ShapeDtypeStruct((cores, queries, rows, tokens), F32)] * len(inputs),
        name="project",
    )(*[x for x, _ in inputs], both, *after)


def tally(where, projected, pieces, early, both, starts, ends, running):
    cores, queries, rows, features = both.shape
    tokens = starts.shape[1]
    block = math.gcd(rows, 512)
    docs = starts.shape[0]
    arrays = []

    def place(array):
        if not any(array is other for other in arrays):
            arrays.append(array)
        return next(i for i, o in enumerate(arrays) if o is array)

    fresh = [(place(x), first) for (x, first), _ in pieces] + [(place(x), f) for x, f in early]
    ready = [place(p) for p, _ in projected]
    grads = [(place(g), f) for _, (g, f) in projected] + [(place(g), f) for _, (g, f) in pieces]
    held, count = len(ready), len(pieces)

    def body(where_ref, *refs):
        p_ref, st_ref, en_ref, run_ref, o_ref = refs[len(arrays) : len(arrays) + 5]
        t_refs = refs[len(arrays) + 5 : len(arrays) + 5 + len(early)]
        x_all = refs[-1]
        for n, (i, first) in enumerate(fresh):
            x_all[:, n * tokens : (n + 1) * tokens] = refs[i][first : first + features, :]
        scores = [[jnp.zeros((1, tokens), F32)] * queries for _ in grads]
        for c in range(cores):
            for q in range(queries):
                for r in range(0, rows, block):
                    if fresh:
                        turned = jnp.dot(
                            p_ref[c, q, r : r + block, :], x_all[...], preferred_element_type=F32
                        )
                    for n, t_ref in enumerate(t_refs):
                        t_ref[c, q, r : r + block, :] = turned[
                            :, (count + n) * tokens : (count + n + 1) * tokens
                        ]
                    for n, (i, first) in enumerate(grads):
                        if n < held:
                            mine = refs[ready[n]][c, q, r : r + block, :]
                        else:
                            mine = turned[:, (n - held) * tokens : (n - held + 1) * tokens]
                        first = first + c * rows + r
                        scores[n][q] = scores[n][q] + jnp.sum(
                            mine * refs[i][first : first + block, :].astype(F32),
                            axis=0,
                            keepdims=True,
                        )
        for q in range(queries):
            total = run_ref[q]
            for n in range(len(grads)):
                spot = where_ref[n] * tokens + lax.broadcasted_iota(jnp.int32, (docs, tokens), 1)
                inside = (spot >= st_ref[...]) & (spot < en_ref[...])
                total = total + jnp.where(inside, scores[n][q], 0.0)
            o_ref[q] = total

    vmem = pl.BlockSpec(memory_space=pltpu.VMEM)
    kept = jax.ShapeDtypeStruct((cores, queries, rows, tokens), F32)
    return call(
        body,
        in_specs=[pl.BlockSpec(memory_space=pltpu.SMEM)]
        + [vmem] * len(arrays)
        + [vmem if fresh else pl.BlockSpec(memory_space=pl.ANY)]
        + [vmem] * 3,
        out_specs=[vmem] * (1 + len(early)),
        out_shape=[jax.ShapeDtypeStruct(running.shape, F32)] + [kept] * len(early),
        scratch_shapes=[pltpu.VMEM((features, len(fresh) * tokens), BF16)] if fresh else [],
        name="tally",
    )(where, *arrays, both, starts, ends, running)


def local_rows(
    depth, layer_inputs, output_grads, query_grads, eigenvalues, out_basis, in_basis, doc_lengths
):
    devices = 4 * depth
    chips = 2 * depth
    tokens = layer_inputs.shape[0]
    queries = query_grads.shape[1]
    entries = output_grads.shape[1] * layer_inputs.shape[1]
    me = lax.axis_index("dp")
    chip = me // 2
    core = me % 2

    def swap(value, offset):
        return lax.ppermute(value, "dp", [(i, i ^ offset) for i in range(devices)])

    features = layer_inputs.shape[1]
    part = output_grads.shape[1] // chips
    turn = functools.partial(rotate, output_grads, out_basis, chip, chips)
    x, side, g_own = turn([[None], [None, 1, 3], [0]], layer_inputs, in_basis)
    far_x = swap(x, 12)
    near_x = swap(x, 4)
    side = swap(side, 2)
    first = [far_x, near_x, side]

    middle, g_far, g_far_side, near_g = turn([[4, 5], [6], [7], [2]])
    sums = sum_eigenvalues(eigenvalues)
    sums = sums + swap(sums, 1)
    sums = hold(sums, middle)
    for offset in (2, 4):
        sums = sums + swap(sums, offset)

    sides_sent, middle = pack([[(near_x, 0, features), (far_x, 0, features)]], [middle], first)
    middle = swap(middle, 8)
    middle_x = swap(far_x, 4)
    sides = swap(sides_sent, 2)
    second = [middle, middle_x, sides]

    sums = hold(sums, sides_sent)
    sums = sums + swap(sums, 8)
    own = precondition_rows(
        query_grads, eigenvalues, sums, out_basis, in_basis, me, entries, first
    )
    both = join_rows(own, swap(own, 1), core, [])

    middle_side, near_g, g_far, g_far_side = pack(
        [
            [(middle_x, 0, features), (middle, part, part)],
            [(near_g, 0, part), (side, features + part, part)],
        ],
        [g_far, g_far_side],
        second + [own],
        COST_K3,
    )
    middle_side = swap(middle_side, 2)
    g_far = swap(g_far, 12)
    g_far_side = swap(g_far_side, 14)
    near_g = swap(near_g, 4)

    doc_ends = jnp.cumsum(doc_lengths)
    doc_starts = doc_ends - doc_lengths
    docs = doc_lengths.shape[0]
    starts = jnp.broadcast_to(doc_starts[:, None], (docs, tokens))
    ends = jnp.broadcast_to(doc_ends[:, None], (docs, tokens))
    running = jnp.zeros((queries, docs, tokens), F32)

    def where(*offsets):
        return jnp.stack([me ^ (2 * k) for k in offsets]).astype(jnp.int32)

    running, *kept = tally(
        where(0, 1, 4),
        [],
        [
            ((x, 0), (g_own, 0)),
            ((side, 0), (side, features)),
            ((middle_x, 0), (middle, 0)),
        ],
        [(near_x, 0), (sides, 0), (far_x, 0), (sides, features)],
        both,
        starts,
        ends,
        running,
    )
    projected = project([(middle_side, 0)], both, tokens, [running])
    (running,) = tally(
        where(2, 3, 6, 7, 5),
        [
            (kept[0], (near_g, 0)),
            (kept[1], (near_g, part)),
            (kept[2], (g_far, 0)),
            (kept[3], (g_far_side, 0)),
            (projected[0], (middle_side, features)),
        ],
        [],
        [],
        both,
        starts,
        ends,
        running,
    )
    shares = jnp.sum(running, axis=2)
    for offset in (1, 2, 4, 8):
        shares = shares + swap(shares, offset)
    each = docs // devices
    mine = lax.dynamic_slice_in_dim(shares, me * each, each, 1)
    return mine.T


def local(layer_inputs, output_grads, query_grads, eigenvalues, out_basis, in_basis, doc_lengths, devices):
    args = (layer_inputs, output_grads, query_grads, eigenvalues, out_basis, in_basis, doc_lengths)
    in_tiles = layer_inputs.shape[1] // query_grads.shape[3]
    tile_count = query_grads.shape[0]
    if devices == 16 and tile_count % in_tiles == 0:
        return local_rows(devices // 4, *args)
    return local_general(*args)


def solution(mesh):
    in_specs = (
        P(("groups", "dp"), None),
        P(("groups", "dp"), None),
        P("dp", None, None, None),
        P("dp", None, None),
        P(),
        P(),
        P("groups"),
    )
    out_specs = P(("groups", "dp"), None)
    body = functools.partial(local, devices=mesh.shape["dp"])
    return jax.shard_map(body, mesh=mesh, in_specs=in_specs, out_specs=out_specs, check_vma=False)
```

```python
import functools
import math

import jax
import jax.numpy as jnp
from jax import lax
from jax.experimental import pallas as pl
from jax.experimental.pallas import tpu as pltpu
from jax.sharding import PartitionSpec as P

VMEM_LIMIT = 16 * 1024 * 1024
COST_PRE = 10**11
COST_K1 = 1
COST_KG = 10**11
COST_K3 = 10**11
F32 = jnp.float32
BF16 = jnp.bfloat16


def turn_rows(columns, basis_blocks):
    group_count = basis_blocks.shape[0]
    block_width = basis_blocks.shape[1]
    grouped = columns.reshape(columns.shape[0], group_count, block_width)
    turned = jnp.einsum("tnk,nkj->tnj", grouped, basis_blocks, preferred_element_type=jnp.float32)
    return turned.reshape(columns.shape).astype(jnp.bfloat16)


def precondition(query_grads, eigenvalues, damping, tile_out, tile_in):
    blocks, queries, rows_out, rows_in = query_grads.shape
    block_width = tile_in.shape[-1]
    grouped = query_grads.reshape(blocks, queries, rows_out, rows_in // block_width, block_width)
    half_turned = jnp.einsum(
        "bqonk,bnkj->bqonj", grouped, tile_in, preferred_element_type=jnp.float32
    )
    half_turned = half_turned.reshape(blocks, queries, rows_out, rows_in).astype(jnp.bfloat16)
    grouped = half_turned.reshape(blocks, queries, rows_out // block_width, block_width, rows_in)
    turned = jnp.einsum("bqnki,bnkj->bqnji", grouped, tile_out, preferred_element_type=jnp.float32)
    turned = turned.reshape(blocks, queries, rows_out, rows_in)
    return (turned / (eigenvalues[:, None] + damping)).astype(jnp.bfloat16)


def tally_scores(grads_got, inputs_got, preconditioned, doc_starts, doc_ends):
    blocks, total_rows, rows_out = grads_got.shape
    queries = preconditioned.shape[1]
    row_step = math.gcd(1024, total_rows)
    flat_pre = preconditioned.reshape(blocks, queries * rows_out, preconditioned.shape[3])

    def one_piece(running, piece_index):
        start_row = piece_index * row_step
        grads_piece = lax.dynamic_slice_in_dim(grads_got, start_row, row_step, 1)
        inputs_piece = lax.dynamic_slice_in_dim(inputs_got, start_row, row_step, 1)
        projected = jnp.einsum(
            "bti,bpi->btp", inputs_piece, flat_pre, preferred_element_type=jnp.float32
        )
        projected = projected.reshape(blocks, row_step, queries, rows_out)
        scores = jnp.sum(projected * grads_piece[:, :, None, :].astype(jnp.float32), axis=(0, 3))
        positions = start_row + lax.iota(jnp.int32, row_step)
        member = (
            (positions[:, None] >= doc_starts[None, :]) & (positions[:, None] < doc_ends[None, :])
        ).astype(jnp.float32)
        added = jnp.einsum("td,tq->dq", member, scores, precision=lax.Precision.HIGHEST)
        return (running + added, None)

    initial = jnp.zeros((doc_starts.shape[0], queries), jnp.float32)
    summed, _ = lax.scan(one_piece, initial, jnp.arange(total_rows // row_step, dtype=jnp.int32))
    return summed


def local_general(
    layer_inputs, output_grads, query_grads, eigenvalues, out_basis, in_basis, doc_lengths
):
    block_width = out_basis.shape[1]
    tok_count = layer_inputs.shape[0]
    tile_count = query_grads.shape[0]
    rows_out = query_grads.shape[2]
    rows_in = query_grads.shape[3]
    in_tiles = layer_inputs.shape[1] // rows_in
    out_tiles = output_grads.shape[1] // rows_out
    tile_ids = lax.axis_index("dp") * tile_count + lax.iota(jnp.int32, tile_count)
    out_sets = out_basis.reshape(out_tiles, rows_out // block_width, block_width, block_width)
    in_sets = in_basis.reshape(in_tiles, rows_in // block_width, block_width, block_width)
    tile_out = jnp.take(out_sets, tile_ids // in_tiles, axis=0)
    tile_in = jnp.take(in_sets, tile_ids % in_tiles, axis=0)
    eigen_sum = lax.psum(jnp.sum(eigenvalues), "dp")
    entries = output_grads.shape[1] * layer_inputs.shape[1]
    damping = 0.1 * (eigen_sum / entries)
    preconditioned = precondition(query_grads, eigenvalues, damping, tile_out, tile_in)
    grads_local = turn_rows(output_grads, out_basis)
    inputs_local = turn_rows(layer_inputs, in_basis)
    grads_tiles = grads_local.reshape(tok_count, out_tiles, rows_out).transpose(1, 0, 2)[:, None]
    grads_tiles = jnp.broadcast_to(grads_tiles, (out_tiles, in_tiles, tok_count, rows_out))
    grads_tiles = grads_tiles.reshape(out_tiles * in_tiles, tok_count, rows_out)
    inputs_tiles = inputs_local.reshape(tok_count, in_tiles, rows_in).transpose(1, 0, 2)[None]
    inputs_tiles = jnp.broadcast_to(inputs_tiles, (out_tiles, in_tiles, tok_count, rows_in))
    inputs_tiles = inputs_tiles.reshape(out_tiles * in_tiles, tok_count, rows_in)
    grads_got, inputs_got = (
        lax.all_to_all(grads_tiles, "dp", split_axis=0, concat_axis=1, tiled=True),
        lax.all_to_all(inputs_tiles, "dp", split_axis=0, concat_axis=1, tiled=True),
    )
    doc_ends = jnp.cumsum(doc_lengths)
    doc_starts = doc_ends - doc_lengths
    partial_scores = tally_scores(grads_got, inputs_got, preconditioned, doc_starts, doc_ends)
    return lax.psum_scatter(partial_scores, "dp", scatter_dimension=0, tiled=True)


def dot_tt(a, b):
    return lax.dot_general(a, b, (((0,), (1,)), ((), ())), preferred_element_type=F32)


def call(body, cost=1, **kw):
    return pl.pallas_call(
        body,
        compiler_params=pltpu.CompilerParams(vmem_limit_bytes=VMEM_LIMIT),
        cost_estimate=pl.CostEstimate(flops=cost, bytes_accessed=1, transcendentals=0),
        **kw,
    )


def in_hbm(value):
    return pltpu.with_memory_space_constraint(value, pltpu.HBM)


def rotate(output_grads, out_basis, chip, chips, layouts, after=(), cost=1):
    tokens, units = output_grads.shape
    width = out_basis.shape[1]
    part = units // chips
    per = part // width
    offsets = [k for layout in layouts for k in layout]
    count = len(offsets)

    def body(chip_ref, g_hbm, b_hbm, *refs):
        o_refs = refs[len(after) : len(after) + len(layouts)]
        g_all, b_all, g_sems, b_sems = refs[len(after) + len(layouts) :]
        copies = []
        for n, k in enumerate(offsets):
            place = chip_ref[0] ^ k
            cols = pl.ds(pl.multiple_of(place * part, part), part)
            blocks = pl.ds(place * per, per)
            copies.append(
                (
                    pltpu.make_async_copy(g_hbm.at[:, cols], g_all.at[n], g_sems.at[n]),
                    pltpu.make_async_copy(b_hbm.at[blocks], b_all.at[n], b_sems.at[n]),
                )
            )
        for pair in copies:
            for copy in pair:
                copy.start()
        n = 0
        for o_ref, layout in zip(o_refs, layouts):
            for top in range(len(layout)):
                for copy in copies[n]:
                    copy.wait()
                for i in range(per):
                    span = slice(i * width, (i + 1) * width)
                    first = top * part + i * width
                    turned = jnp.dot(g_all[n, :, span], b_all[n, i], preferred_element_type=F32)
                    o_ref[first : first + width, :] = turned.astype(BF16).T
                n += 1

    hbm = pl.BlockSpec(memory_space=pl.ANY)
    vmem = pl.BlockSpec(memory_space=pltpu.VMEM)
    return call(
        body,
        cost=cost,
        in_specs=[pl.BlockSpec(memory_space=pltpu.SMEM), hbm, hbm] + [hbm] * len(after),
        out_specs=[vmem] * len(layouts),
        out_shape=[jax.ShapeDtypeStruct((part * len(l), tokens), BF16) for l in layouts],
        scratch_shapes=[
            pltpu.VMEM((count, tokens, part), BF16),
            pltpu.VMEM((count, per, width, width), BF16),
            pltpu.SemaphoreType.DMA((count,)),
            pltpu.SemaphoreType.DMA((count,)),
        ],
        name="rotate",
    )(chip[None], in_hbm(output_grads), in_hbm(out_basis), *after)


def turn(x_ref, first, tokens, basis_ref, o_ref, left=0, cut=None, rest_ref=None):
    count, width, _ = basis_ref.shape
    for i in range(count):
        span = slice(i * width, (i + 1) * width)
        turned = jnp.dot(
            x_ref[first : first + tokens, span], basis_ref[i], preferred_element_type=F32
        )
        turned = turned.astype(BF16).T
        if cut is None or i * width < cut:
            o_ref[span, left : left + tokens] = turned
        else:
            rest_ref[i * width - cut : (i + 1) * width - cut, :] = turned


def pair_up(a, b, held, after):
    def body(a_ref, b_ref, *refs):
        o_ref = refs[1 + len(after)]
        o_ref[: a.shape[0], :] = a_ref[...]
        o_ref[a.shape[0] :, :] = b_ref[...]

    anywhere = pl.BlockSpec(memory_space=pl.ANY)
    vmem = pl.BlockSpec(memory_space=pltpu.VMEM)
    return call(
        body,
        in_specs=[vmem, vmem] + [anywhere] * (1 + len(after)),
        out_specs=[vmem, anywhere],
        out_shape=[
            jax.ShapeDtypeStruct((a.shape[0] + b.shape[0], a.shape[1]), a.dtype),
            jax.ShapeDtypeStruct(held.shape, held.dtype),
        ],
        input_output_aliases={2: 1},
        name="pair_up",
    )(a, b, held, *after)


def pack_grads(near, far, across):
    part, tokens = near.shape

    def body(n_ref, f_ref, a_ref, near_ref, far_ref, sems):
        top, low = pl.ds(0, part), pl.ds(part, part)
        copies = [
            pltpu.make_async_copy(n_ref, near_ref.at[top], sems.at[0]),
            pltpu.make_async_copy(a_ref.at[low], near_ref.at[low], sems.at[1]),
            pltpu.make_async_copy(f_ref, far_ref.at[top], sems.at[2]),
            pltpu.make_async_copy(a_ref.at[pl.ds(2 * part, part)], far_ref.at[low], sems.at[3]),
        ]
        for copy in copies:
            copy.start()
        for copy in copies:
            copy.wait()

    anywhere = pl.BlockSpec(memory_space=pl.ANY)
    vmem = pl.BlockSpec(memory_space=pltpu.VMEM)
    return call(
        body,
        in_specs=[anywhere] * 3,
        out_specs=[vmem] * 2,
        out_shape=[jax.ShapeDtypeStruct((2 * part, tokens), BF16)] * 2,
        scratch_shapes=[pltpu.SemaphoreType.DMA((4,))],
        name="pack_grads",
    )(near, far, across)


def last_round(x, middle, in_basis, cut, after):
    tokens = x.shape[0]
    count, width, _ = in_basis.shape
    features = count * width
    part = middle.shape[0] // 2

    def body(x_ref, m_ref, b_ref, *refs):
        high_ref, low_ref, sem = refs[len(after) :]
        copy = pltpu.make_async_copy(
            m_ref.at[pl.ds(part, part)], low_ref.at[pl.ds(features - cut, part)], sem
        )
        copy.start()
        turn(x_ref, 0, tokens, b_ref, high_ref, 0, cut, low_ref)
        copy.wait()

    anywhere = pl.BlockSpec(memory_space=pl.ANY)
    vmem = pl.BlockSpec(memory_space=pltpu.VMEM)
    return call(
        body,
        cost=COST_K3,
        in_specs=[vmem, anywhere, vmem] + [anywhere] * len(after),
        out_specs=[vmem] * 2,
        out_shape=[
            jax.ShapeDtypeStruct((cut, tokens), BF16),
            jax.ShapeDtypeStruct((features - cut + part, tokens), BF16),
        ],
        scratch_shapes=[pltpu.SemaphoreType.DMA],
        name="last_round",
    )(x, middle, in_basis, *after)


def sum_eigenvalues(eigenvalues):
    tiles, rows, cols = eigenvalues.shape

    def body(e_ref, o_ref):
        @pl.when(pl.program_id(0) == 0)
        def _():
            o_ref[...] = jnp.zeros_like(o_ref)

        part = jnp.sum(e_ref[0].reshape(rows // 8, 8, cols), axis=0)
        total = part[:, :128]
        for n in range(1, cols // 128):
            total = total + part[:, n * 128 : (n + 1) * 128]
        o_ref[...] += total

    return call(
        body,
        grid=(tiles,),
        in_specs=[pl.BlockSpec((1, rows, cols), lambda b: (b, 0, 0))],
        out_specs=pl.BlockSpec((8, 128), lambda b: (0, 0)),
        out_shape=jax.ShapeDtypeStruct((8, 128), F32),
        name="sum_eigenvalues",
    )(eigenvalues)


def hold(value, *after):
    def body(v_ref, *refs):
        refs[-1][...] = v_ref[...]

    vmem = pl.BlockSpec(memory_space=pltpu.VMEM)
    return call(
        body,
        in_specs=[vmem] + [pl.BlockSpec(memory_space=pl.ANY)] * len(after),
        out_specs=vmem,
        out_shape=jax.ShapeDtypeStruct(value.shape, value.dtype),
        name="hold",
    )(value, *after)


def block_diagonal(blocks):
    count, width = len(blocks), blocks[0].shape[0]
    zero = jnp.zeros((width, width), blocks[0].dtype)
    rows = [
        jnp.concatenate([blocks[i] if i == j else zero for j in range(count)], axis=1)
        for i in range(count)
    ]
    return jnp.concatenate(rows, axis=0)


def precondition_rows(query_grads, eigenvalues, sums, out_basis, in_basis, me, entries, after):
    tiles, queries, rows, cols = query_grads.shape
    width = in_basis.shape[1]
    features = in_basis.shape[0] * width
    in_tiles = features // cols
    groups = tiles // in_tiles
    n_out, n_in = rows // width, cols // width
    pair = 2 if n_out % 2 == 0 else 1
    span = pair * width

    def body(me_ref, q_ref, e_ref, s_ref, ob_ref, ib_ref, *refs):
        o_ref, turn_ref = refs[len(after) :]

        @pl.when(pl.program_id(0) % in_tiles == 0)
        def _():
            for n in range(n_out // pair):
                turn_ref[n] = block_diagonal([ob_ref[n * pair + k].T for k in range(pair)])

        damping = 0.1 * (jnp.sum(s_ref[...], keepdims=True) / entries)
        scale = 1.0 / (e_ref[0] + damping)
        half = jnp.dot(
            q_ref[0].reshape(queries * rows, cols),
            block_diagonal([ib_ref[n] for n in range(n_in)]),
            preferred_element_type=F32,
        ).astype(BF16)
        for q in range(queries):
            for n in range(n_out // pair):
                start = n * span
                turned = jnp.dot(
                    turn_ref[n],
                    half[q * rows + start : q * rows + start + span],
                    preferred_element_type=F32,
                )
                o_ref[q, start : start + span, :] = (turned * scale[start : start + span]).astype(
                    BF16
                )

    grid_spec = pltpu.PrefetchScalarGridSpec(
        num_scalar_prefetch=1,
        grid=(tiles,),
        in_specs=[
            pl.BlockSpec((1, queries, rows, cols), lambda b, m: (b, 0, 0, 0)),
            pl.BlockSpec((1, rows, cols), lambda b, m: (b, 0, 0)),
            pl.BlockSpec(sums.shape, lambda b, m: (0, 0)),
            pl.BlockSpec((n_out, width, width), lambda b, m: (m[0] * groups + b // in_tiles, 0, 0)),
            pl.BlockSpec((n_in, width, width), lambda b, m: (b % in_tiles, 0, 0)),
        ]
        + [pl.BlockSpec(memory_space=pl.ANY)] * len(after),
        out_specs=pl.BlockSpec(
            (queries, rows, cols), lambda b, m: (0, b // in_tiles, b % in_tiles)
        ),
        scratch_shapes=[pltpu.VMEM((n_out // pair, span, span), BF16)],
    )
    return call(
        body,
        grid_spec=grid_spec,
        out_shape=jax.ShapeDtypeStruct((queries, groups * rows, features), BF16),
        name="precondition",
        cost=COST_PRE,
    )(me[None], query_grads, eigenvalues, sums, out_basis, in_basis, *after)


def join_and_tally(where, turned_piece, pieces, early, in_basis, own, sibling, starts, ends, order):
    queries, rows, features = own.shape
    docs, tokens = starts.shape
    width = in_basis.shape[1]
    block = math.gcd(rows, 512)
    all_pieces = [turned_piece] + list(pieces)
    count = len(all_pieces)
    raw = [x for x, _ in pieces] + list(early)
    cut = turned_piece[0][0].shape[0]
    raw_place = [next(i for i, o in enumerate(order) if o is x) for x, _ in raw]
    heights = [array.shape[0] for array in order]
    tops = [sum(heights[:i]) for i in range(len(heights))]
    grads = [g for _, (g, _) in all_pieces]
    operands = list(order) + [in_hbm(in_basis), *turned_piece[0]]
    operands += [in_hbm(g) for g in grads] + [own, sibling, starts, ends]

    def body(where_ref, *refs):
        raw_refs = refs[: len(order)]
        basis_hbm, high_hbm, low_hbm = refs[len(order) : len(order) + 3]
        g_hbm = refs[len(order) + 3 : len(order) + 3 + count]
        own_ref, sib_ref, st_ref, en_ref, o_ref, both_ref = refs[
            len(order) + 3 + count : len(operands) + 2
        ]
        t_refs = refs[len(operands) + 2 : -7]
        raw_all, basis_ref, x_all, g_all, x_sems, g_sems, p_sems = refs[-7:]
        x_copies = [pltpu.make_async_copy(basis_hbm, basis_ref, x_sems.at[len(order)])]
        x_copies += [
            pltpu.make_async_copy(
                raw_refs[i], raw_all.at[pl.ds(tops[i], heights[i])], x_sems.at[i]
            )
            for i in range(len(order))
        ]
        copies = [
            [
                pltpu.make_async_copy(p_ref.at[q], both_ref.at[c, q], p_sems.at[c, q])
                for q in range(queries)
            ]
            for c, p_ref in enumerate((own_ref, sib_ref))
        ]
        x_copies += [
            pltpu.make_async_copy(
                high_hbm, x_all.at[pl.ds(0, cut), pl.ds(0, tokens)], x_sems.at[len(order) + 1]
            ),
            pltpu.make_async_copy(
                low_hbm.at[pl.ds(0, features - cut)],
                x_all.at[pl.ds(cut, features - cut), pl.ds(0, tokens)],
                x_sems.at[len(order) + 2],
            ),
        ]
        g_copies = [
            pltpu.make_async_copy(
                g_hbm[n].at[pl.ds(all_pieces[n][1][1], 2 * rows)], g_all.at[n], g_sems.at[n]
            )
            for n in range(count)
        ]
        for copy in x_copies:
            copy.start()
        copies[0][0].start()
        for copy in g_copies:
            copy.start()
        for c in range(2):
            for q in range(queries):
                if c or q:
                    copies[c][q].start()
        for copy in x_copies:
            copy.wait()
        for n, (_, first) in enumerate(raw):
            turn(raw_all, tops[raw_place[n]] + first, tokens, basis_ref, x_all, (n + 1) * tokens)
        scores = [[jnp.zeros((1, tokens), F32)] * queries for _ in all_pieces]
        for c in range(2):
            core = where_ref[0] if c == 0 else 1 - where_ref[0]
            for q in range(queries):
                copies[c][q].wait()
                if c == 0 and q == 0:
                    for copy in g_copies:
                        copy.wait()
                for r in range(0, rows, block):
                    turned = jnp.dot(
                        both_ref[c, q, r : r + block, :], x_all[...], preferred_element_type=F32
                    )
                    for n, t_ref in enumerate(t_refs):
                        left = (count + n) * tokens
                        t_ref[c, q, r : r + block, :] = turned[:, left : left + tokens]
                    for n in range(count):
                        spot = pl.ds(pl.multiple_of(core * rows + r, block), block)
                        scores[n][q] = scores[n][q] + jnp.sum(
                            turned[:, n * tokens : (n + 1) * tokens]
                            * g_all[n, spot, :].astype(F32),
                            axis=0,
                            keepdims=True,
                        )
        add_shares(where_ref, scores, None, st_ref, en_ref, o_ref)

    hbm = pl.BlockSpec(memory_space=pl.ANY)
    vmem = pl.BlockSpec(memory_space=pltpu.VMEM)
    kept = jax.ShapeDtypeStruct((2, queries, rows, tokens), F32)
    return call(
        body,
        in_specs=[pl.BlockSpec(memory_space=pltpu.SMEM)]
        + [hbm] * (len(order) + 3 + count)
        + [hbm, hbm, vmem, vmem],
        out_specs=[vmem] * (2 + len(early)),
        out_shape=[
            jax.ShapeDtypeStruct((queries, docs, tokens), F32),
            jax.ShapeDtypeStruct((2,) + own.shape, own.dtype),
        ]
        + [kept] * len(early),
        scratch_shapes=[
            pltpu.VMEM((sum(heights), features), BF16),
            pltpu.VMEM(in_basis.shape, BF16),
            pltpu.VMEM((features, (count + len(early)) * tokens), BF16),
            pltpu.VMEM((count, 2 * rows, tokens), BF16),
            pltpu.SemaphoreType.DMA((len(order) + 3,)),
            pltpu.SemaphoreType.DMA((count,)),
            pltpu.SemaphoreType.DMA((2, queries)),
        ],
        name="join_and_tally",
    )(where, *operands)


def add_shares(where_ref, scores, run_ref, st_ref, en_ref, o_ref):
    docs, tokens = st_ref.shape
    for q in range(len(scores[0])):
        total = jnp.zeros((docs, tokens), F32) if run_ref is None else run_ref[q]
        for n in range(len(scores)):
            spot = where_ref[1 + n] * tokens + lax.broadcasted_iota(jnp.int32, (docs, tokens), 1)
            inside = (spot >= st_ref[...]) & (spot < en_ref[...])
            total = total + jnp.where(inside, scores[n][q], 0.0)
        o_ref[q] = total


def project(high, low, both, after):
    cores, queries, rows, features = both.shape
    cut, tokens = high.shape
    block = math.gcd(rows, 512)

    def body(h_ref, l_ref, p_ref, *refs):
        x_all = refs[-1]
        x_all[:cut, :] = h_ref[...]
        x_all[cut:, :] = l_ref[: features - cut, :]
        for c in range(cores):
            for q in range(queries):
                for r in range(0, rows, block):
                    span = slice(r, r + block)
                    refs[-2][c, q, span, :] = jnp.dot(
                        p_ref[c, q, span, :], x_all[...], preferred_element_type=F32
                    )

    vmem = pl.BlockSpec(memory_space=pltpu.VMEM)
    return call(
        body,
        in_specs=[vmem] * 3 + [pl.BlockSpec(memory_space=pl.ANY)] * len(after),
        out_specs=vmem,
        out_shape=jax.ShapeDtypeStruct((cores, queries, rows, tokens), F32),
        scratch_shapes=[pltpu.VMEM((features, tokens), BF16)],
        name="project",
    )(high, low, both, *after)


def tally(where, projected, grads, starts, ends, running, order):
    cores, queries, rows, tokens = projected[0].shape
    block = math.gcd(rows, 512)
    arrays = list(order)
    places = [next(i for i, o in enumerate(arrays) if o is array) for array, _ in grads]
    held = len(projected)

    def body(where_ref, *refs):
        g_refs = refs[held : held + len(arrays)]
        st_ref, en_ref, run_ref, o_ref = refs[held + len(arrays) :]
        scores = [[jnp.zeros((1, tokens), F32)] * queries for _ in grads]
        for c in range(cores):
            core = where_ref[0] if c == 0 else 1 - where_ref[0]
            for q in range(queries):
                for r in range(0, rows, block):
                    for n, (_, first) in enumerate(grads):
                        spot = pl.ds(pl.multiple_of(core * rows + first + r, block), block)
                        scores[n][q] = scores[n][q] + jnp.sum(
                            refs[n][c, q, r : r + block, :]
                            * g_refs[places[n]][spot, :].astype(F32),
                            axis=0,
                            keepdims=True,
                        )
        add_shares(where_ref, scores, run_ref, st_ref, en_ref, o_ref)

    vmem = pl.BlockSpec(memory_space=pltpu.VMEM)
    return call(
        body,
        in_specs=[pl.BlockSpec(memory_space=pltpu.SMEM)] + [vmem] * (held + len(arrays) + 3),
        out_specs=vmem,
        out_shape=jax.ShapeDtypeStruct(running.shape, F32),
        name="tally",
    )(where, *projected, *arrays, starts, ends, running)


def local_rows(
    depth, layer_inputs, output_grads, query_grads, eigenvalues, out_basis, in_basis, doc_lengths
):
    devices = 4 * depth
    chips = 2 * depth
    tokens = layer_inputs.shape[0]
    queries = query_grads.shape[1]
    entries = output_grads.shape[1] * layer_inputs.shape[1]
    me = lax.axis_index("dp")
    chip = me // 2
    core = me % 2

    def swap(value, offset):
        return lax.ppermute(value, "dp", [(i, i ^ offset) for i in range(devices)])

    features = layer_inputs.shape[1]
    part = output_grads.shape[1] // chips
    spin = functools.partial(rotate, output_grads, out_basis, chip, chips)
    far_x = swap(layer_inputs, 12)
    near_x = swap(layer_inputs, 4)
    side_x = swap(layer_inputs, 2)
    sums = sum_eigenvalues(eigenvalues)
    (side_g,) = spin([[1, 3, 7]], [sums], cost=COST_K1)
    side_g = swap(side_g, 2)

    g_own, middle, g_far, near_g = spin([[0], [4, 5], [6], [2]], cost=COST_KG)
    sums = sums + swap(sums, 2)
    sums = hold(sums, middle)
    for offset in (1, 4):
        sums = sums + swap(sums, offset)

    sides_sent, middle = pair_up(near_x, far_x, middle, [side_x])
    middle = swap(middle, 8)
    middle_x = swap(far_x, 4)
    sides = swap(sides_sent, 2)

    sums = hold(sums, sides_sent)
    sums = sums + swap(sums, 8)
    own = precondition_rows(
        query_grads, eigenvalues, sums, out_basis, in_basis, me, entries, [near_x, far_x, side_x, side_g]
    )
    sibling = swap(own, 1)

    near_g, g_far = pack_grads(near_g, g_far, side_g)
    near_g = swap(near_g, 4)
    g_far = swap(g_far, 12)
    cut = features * 3 // 4
    turned = last_round(middle_x, middle, in_basis, cut, [sides, own])
    high, low = [swap(value, 2) for value in turned]

    doc_ends = jnp.cumsum(doc_lengths)
    doc_starts = doc_ends - doc_lengths
    docs = doc_lengths.shape[0]
    starts = jnp.broadcast_to(doc_starts[:, None], (docs, tokens))
    ends = jnp.broadcast_to(doc_ends[:, None], (docs, tokens))

    def where(*offsets):
        return jnp.stack([core] + [me ^ (2 * k) for k in offsets]).astype(jnp.int32)

    layer_inputs = in_hbm(layer_inputs)
    running, both, *kept = join_and_tally(
        where(4, 0, 1),
        (turned, (middle, 0)),
        [((layer_inputs, 0), (g_own, 0)), ((side_x, 0), (side_g, 0))],
        [(near_x, 0), (sides, 0), (far_x, 0), (sides, tokens)],
        in_basis,
        own,
        sibling,
        starts,
        ends,
        [layer_inputs, side_x, near_x, far_x, sides],
    )
    kept.append(project(high, low, both, [running]))
    running = tally(
        where(2, 3, 6, 7, 5),
        kept,
        [(near_g, 0), (near_g, part), (g_far, 0), (g_far, part), (low, features - cut)],
        starts,
        ends,
        running,
        [near_g, g_far, low],
    )
    shares = jnp.sum(running, axis=2)
    for offset in (1, 2, 4, 8):
        shares = shares + swap(shares, offset)
    each = docs // devices
    mine = lax.dynamic_slice_in_dim(shares, me * each, each, 1)
    return mine.T


def local(layer_inputs, output_grads, query_grads, eigenvalues, out_basis, in_basis, doc_lengths, devices):
    args = (layer_inputs, output_grads, query_grads, eigenvalues, out_basis, in_basis, doc_lengths)
    in_tiles = layer_inputs.shape[1] // query_grads.shape[3]
    tile_count = query_grads.shape[0]
    if devices == 16 and tile_count % in_tiles == 0:
        return local_rows(devices // 4, *args)
    return local_general(*args)


def solution(mesh):
    in_specs = (
        P(("groups", "dp"), None),
        P(("groups", "dp"), None),
        P("dp", None, None, None),
        P("dp", None, None),
        P(),
        P(),
        P("groups"),
    )
    out_specs = P(("groups", "dp"), None)
    body = functools.partial(local, devices=mesh.shape["dp"])
    return jax.shard_map(body, mesh=mesh, in_specs=in_specs, out_specs=out_specs, check_vma=False)
```

```python
import functools
import math

import jax
import jax.numpy as jnp
from jax import lax
from jax.experimental import pallas as pl
from jax.experimental.pallas import tpu as pltpu
from jax.sharding import PartitionSpec as P

VMEM_LIMIT = 16 * 1024 * 1024
COST_PRE = 10**11
COST_K1 = 1
COST_KG = 10**11
COST_K3 = 10**11
F32 = jnp.float32
BF16 = jnp.bfloat16


def turn_rows(columns, basis_blocks):
    group_count = basis_blocks.shape[0]
    block_width = basis_blocks.shape[1]
    grouped = columns.reshape(columns.shape[0], group_count, block_width)
    turned = jnp.einsum("tnk,nkj->tnj", grouped, basis_blocks, preferred_element_type=jnp.float32)
    return turned.reshape(columns.shape).astype(jnp.bfloat16)


def precondition(query_grads, eigenvalues, damping, tile_out, tile_in):
    blocks, queries, rows_out, rows_in = query_grads.shape
    block_width = tile_in.shape[-1]
    grouped = query_grads.reshape(blocks, queries, rows_out, rows_in // block_width, block_width)
    half_turned = jnp.einsum(
        "bqonk,bnkj->bqonj", grouped, tile_in, preferred_element_type=jnp.float32
    )
    half_turned = half_turned.reshape(blocks, queries, rows_out, rows_in).astype(jnp.bfloat16)
    grouped = half_turned.reshape(blocks, queries, rows_out // block_width, block_width, rows_in)
    turned = jnp.einsum("bqnki,bnkj->bqnji", grouped, tile_out, preferred_element_type=jnp.float32)
    turned = turned.reshape(blocks, queries, rows_out, rows_in)
    return (turned / (eigenvalues[:, None] + damping)).astype(jnp.bfloat16)


def tally_scores(grads_got, inputs_got, preconditioned, doc_starts, doc_ends):
    blocks, total_rows, rows_out = grads_got.shape
    queries = preconditioned.shape[1]
    row_step = math.gcd(1024, total_rows)
    flat_pre = preconditioned.reshape(blocks, queries * rows_out, preconditioned.shape[3])

    def one_piece(running, piece_index):
        start_row = piece_index * row_step
        grads_piece = lax.dynamic_slice_in_dim(grads_got, start_row, row_step, 1)
        inputs_piece = lax.dynamic_slice_in_dim(inputs_got, start_row, row_step, 1)
        projected = jnp.einsum(
            "bti,bpi->btp", inputs_piece, flat_pre, preferred_element_type=jnp.float32
        )
        projected = projected.reshape(blocks, row_step, queries, rows_out)
        scores = jnp.sum(projected * grads_piece[:, :, None, :].astype(jnp.float32), axis=(0, 3))
        positions = start_row + lax.iota(jnp.int32, row_step)
        member = (
            (positions[:, None] >= doc_starts[None, :]) & (positions[:, None] < doc_ends[None, :])
        ).astype(jnp.float32)
        added = jnp.einsum("td,tq->dq", member, scores, precision=lax.Precision.HIGHEST)
        return (running + added, None)

    initial = jnp.zeros((doc_starts.shape[0], queries), jnp.float32)
    summed, _ = lax.scan(one_piece, initial, jnp.arange(total_rows // row_step, dtype=jnp.int32))
    return summed


def local_general(
    layer_inputs, output_grads, query_grads, eigenvalues, out_basis, in_basis, doc_lengths
):
    block_width = out_basis.shape[1]
    tok_count = layer_inputs.shape[0]
    tile_count = query_grads.shape[0]
    rows_out = query_grads.shape[2]
    rows_in = query_grads.shape[3]
    in_tiles = layer_inputs.shape[1] // rows_in
    out_tiles = output_grads.shape[1] // rows_out
    tile_ids = lax.axis_index("dp") * tile_count + lax.iota(jnp.int32, tile_count)
    out_sets = out_basis.reshape(out_tiles, rows_out // block_width, block_width, block_width)
    in_sets = in_basis.reshape(in_tiles, rows_in // block_width, block_width, block_width)
    tile_out = jnp.take(out_sets, tile_ids // in_tiles, axis=0)
    tile_in = jnp.take(in_sets, tile_ids % in_tiles, axis=0)
    eigen_sum = lax.psum(jnp.sum(eigenvalues), "dp")
    entries = output_grads.shape[1] * layer_inputs.shape[1]
    damping = 0.1 * (eigen_sum / entries)
    preconditioned = precondition(query_grads, eigenvalues, damping, tile_out, tile_in)
    grads_local = turn_rows(output_grads, out_basis)
    inputs_local = turn_rows(layer_inputs, in_basis)
    grads_tiles = grads_local.reshape(tok_count, out_tiles, rows_out).transpose(1, 0, 2)[:, None]
    grads_tiles = jnp.broadcast_to(grads_tiles, (out_tiles, in_tiles, tok_count, rows_out))
    grads_tiles = grads_tiles.reshape(out_tiles * in_tiles, tok_count, rows_out)
    inputs_tiles = inputs_local.reshape(tok_count, in_tiles, rows_in).transpose(1, 0, 2)[None]
    inputs_tiles = jnp.broadcast_to(inputs_tiles, (out_tiles, in_tiles, tok_count, rows_in))
    inputs_tiles = inputs_tiles.reshape(out_tiles * in_tiles, tok_count, rows_in)
    grads_got, inputs_got = (
        lax.all_to_all(grads_tiles, "dp", split_axis=0, concat_axis=1, tiled=True),
        lax.all_to_all(inputs_tiles, "dp", split_axis=0, concat_axis=1, tiled=True),
    )
    doc_ends = jnp.cumsum(doc_lengths)
    doc_starts = doc_ends - doc_lengths
    partial_scores = tally_scores(grads_got, inputs_got, preconditioned, doc_starts, doc_ends)
    return lax.psum_scatter(partial_scores, "dp", scatter_dimension=0, tiled=True)


def dot_tt(a, b):
    return lax.dot_general(a, b, (((0,), (1,)), ((), ())), preferred_element_type=F32)


def call(body, cost=1, **kw):
    return pl.pallas_call(
        body,
        compiler_params=pltpu.CompilerParams(vmem_limit_bytes=VMEM_LIMIT),
        cost_estimate=pl.CostEstimate(flops=cost, bytes_accessed=1, transcendentals=0),
        **kw,
    )


def in_hbm(value):
    return pltpu.with_memory_space_constraint(value, pltpu.HBM)


def rotate(output_grads, out_basis, chip, chips, layouts, after=(), cost=1):
    tokens, units = output_grads.shape
    width = out_basis.shape[1]
    part = units // chips
    per = part // width
    offsets = [k for layout in layouts for k in layout]
    count = len(offsets)

    def body(chip_ref, g_hbm, b_hbm, *refs):
        o_refs = refs[len(after) : len(after) + len(layouts)]
        g_all, b_all, g_sems, b_sems = refs[len(after) + len(layouts) :]
        copies = []
        for n, k in enumerate(offsets):
            place = chip_ref[0] ^ k
            cols = pl.ds(pl.multiple_of(place * part, part), part)
            blocks = pl.ds(place * per, per)
            copies.append(
                (
                    pltpu.make_async_copy(g_hbm.at[:, cols], g_all.at[n], g_sems.at[n]),
                    pltpu.make_async_copy(b_hbm.at[blocks], b_all.at[n], b_sems.at[n]),
                )
            )
        for pair in copies:
            for copy in pair:
                copy.start()
        n = 0
        for o_ref, layout in zip(o_refs, layouts):
            for top in range(len(layout)):
                for copy in copies[n]:
                    copy.wait()
                for i in range(per):
                    span = slice(i * width, (i + 1) * width)
                    first = top * part + i * width
                    turned = jnp.dot(g_all[n, :, span], b_all[n, i], preferred_element_type=F32)
                    o_ref[first : first + width, :] = turned.astype(BF16).T
                n += 1

    hbm = pl.BlockSpec(memory_space=pl.ANY)
    vmem = pl.BlockSpec(memory_space=pltpu.VMEM)
    return call(
        body,
        cost=cost,
        in_specs=[pl.BlockSpec(memory_space=pltpu.SMEM), hbm, hbm] + [hbm] * len(after),
        out_specs=[vmem] * len(layouts),
        out_shape=[jax.ShapeDtypeStruct((part * len(l), tokens), BF16) for l in layouts],
        scratch_shapes=[
            pltpu.VMEM((count, tokens, part), BF16),
            pltpu.VMEM((count, per, width, width), BF16),
            pltpu.SemaphoreType.DMA((count,)),
            pltpu.SemaphoreType.DMA((count,)),
        ],
        name="rotate",
    )(chip[None], in_hbm(output_grads), in_hbm(out_basis), *after)


def turn(x_ref, first, tokens, basis_ref, o_ref, left=0, cut=None, rest_ref=None):
    count, width, _ = basis_ref.shape
    for i in range(count):
        span = slice(i * width, (i + 1) * width)
        turned = jnp.dot(
            x_ref[first : first + tokens, span], basis_ref[i], preferred_element_type=F32
        )
        turned = turned.astype(BF16).T
        if cut is None or i * width < cut:
            o_ref[span, left : left + tokens] = turned
        else:
            rest_ref[i * width - cut : (i + 1) * width - cut, :] = turned


def pair_up(a, b, held, after):
    def body(a_ref, b_ref, *refs):
        o_ref = refs[1 + len(after)]
        o_ref[: a.shape[0], :] = a_ref[...]
        o_ref[a.shape[0] :, :] = b_ref[...]

    anywhere = pl.BlockSpec(memory_space=pl.ANY)
    vmem = pl.BlockSpec(memory_space=pltpu.VMEM)
    return call(
        body,
        in_specs=[vmem, vmem] + [anywhere] * (1 + len(after)),
        out_specs=[vmem, anywhere],
        out_shape=[
            jax.ShapeDtypeStruct((a.shape[0] + b.shape[0], a.shape[1]), a.dtype),
            jax.ShapeDtypeStruct(held.shape, held.dtype),
        ],
        input_output_aliases={2: 1},
        name="pair_up",
    )(a, b, held, *after)


def pack_grads(near, far, across):
    part, tokens = near.shape

    def body(n_ref, f_ref, a_ref, near_ref, far_ref, sems):
        top, low = pl.ds(0, part), pl.ds(part, part)
        copies = [
            pltpu.make_async_copy(n_ref, near_ref.at[top], sems.at[0]),
            pltpu.make_async_copy(a_ref.at[low], near_ref.at[low], sems.at[1]),
            pltpu.make_async_copy(f_ref, far_ref.at[top], sems.at[2]),
            pltpu.make_async_copy(a_ref.at[pl.ds(2 * part, part)], far_ref.at[low], sems.at[3]),
        ]
        for copy in copies:
            copy.start()
        for copy in copies:
            copy.wait()

    anywhere = pl.BlockSpec(memory_space=pl.ANY)
    vmem = pl.BlockSpec(memory_space=pltpu.VMEM)
    return call(
        body,
        in_specs=[anywhere] * 3,
        out_specs=[vmem] * 2,
        out_shape=[jax.ShapeDtypeStruct((2 * part, tokens), BF16)] * 2,
        scratch_shapes=[pltpu.SemaphoreType.DMA((4,))],
        name="pack_grads",
    )(near, far, across)


def last_round(x, middle, in_basis, cut, after):
    tokens = x.shape[0]
    count, width, _ = in_basis.shape
    features = count * width
    part = middle.shape[0] // 2

    def body(x_ref, m_ref, b_ref, *refs):
        high_ref, low_ref, sem = refs[len(after) :]
        copy = pltpu.make_async_copy(
            m_ref.at[pl.ds(part, part)], low_ref.at[pl.ds(features - cut, part)], sem
        )
        copy.start()
        turn(x_ref, 0, tokens, b_ref, high_ref, 0, cut, low_ref)
        copy.wait()

    anywhere = pl.BlockSpec(memory_space=pl.ANY)
    vmem = pl.BlockSpec(memory_space=pltpu.VMEM)
    return call(
        body,
        cost=COST_K3,
        in_specs=[vmem, anywhere, vmem] + [anywhere] * len(after),
        out_specs=[vmem] * 2,
        out_shape=[
            jax.ShapeDtypeStruct((cut, tokens), BF16),
            jax.ShapeDtypeStruct((features - cut + part, tokens), BF16),
        ],
        scratch_shapes=[pltpu.SemaphoreType.DMA],
        name="last_round",
    )(x, middle, in_basis, *after)


def sum_eigenvalues(eigenvalues):
    tiles, rows, cols = eigenvalues.shape

    def body(e_ref, o_ref):
        @pl.when(pl.program_id(0) == 0)
        def _():
            o_ref[...] = jnp.zeros_like(o_ref)

        part = jnp.sum(e_ref[0].reshape(rows // 8, 8, cols), axis=0)
        total = part[:, :128]
        for n in range(1, cols // 128):
            total = total + part[:, n * 128 : (n + 1) * 128]
        o_ref[...] += total

    return call(
        body,
        grid=(tiles,),
        in_specs=[pl.BlockSpec((1, rows, cols), lambda b: (b, 0, 0))],
        out_specs=pl.BlockSpec((8, 128), lambda b: (0, 0)),
        out_shape=jax.ShapeDtypeStruct((8, 128), F32),
        name="sum_eigenvalues",
    )(eigenvalues)


def hold(value, *after):
    def body(v_ref, *refs):
        refs[-1][...] = v_ref[...]

    vmem = pl.BlockSpec(memory_space=pltpu.VMEM)
    return call(
        body,
        in_specs=[vmem] + [pl.BlockSpec(memory_space=pl.ANY)] * len(after),
        out_specs=vmem,
        out_shape=jax.ShapeDtypeStruct(value.shape, value.dtype),
        name="hold",
    )(value, *after)


def block_diagonal(blocks):
    count, width = len(blocks), blocks[0].shape[0]
    zero = jnp.zeros((width, width), blocks[0].dtype)
    rows = [
        jnp.concatenate([blocks[i] if i == j else zero for j in range(count)], axis=1)
        for i in range(count)
    ]
    return jnp.concatenate(rows, axis=0)


def precondition_rows(query_grads, eigenvalues, sums, out_basis, in_basis, me, entries, after):
    tiles, queries, rows, cols = query_grads.shape
    width = in_basis.shape[1]
    features = in_basis.shape[0] * width
    in_tiles = features // cols
    groups = tiles // in_tiles
    n_out, n_in = rows // width, cols // width
    pair = 2 if n_out % 2 == 0 else 1
    span = pair * width

    def body(me_ref, q_ref, e_ref, s_ref, ob_ref, ib_ref, *refs):
        o_ref, turn_ref = refs[len(after) :]

        @pl.when(pl.program_id(0) % in_tiles == 0)
        def _():
            for n in range(n_out // pair):
                turn_ref[n] = block_diagonal([ob_ref[n * pair + k].T for k in range(pair)])

        damping = 0.1 * (jnp.sum(s_ref[...], keepdims=True) / entries)
        scale = 1.0 / (e_ref[0] + damping)
        half = jnp.dot(
            q_ref[0].reshape(queries * rows, cols),
            block_diagonal([ib_ref[n] for n in range(n_in)]),
            preferred_element_type=F32,
        ).astype(BF16)
        for q in range(queries):
            for n in range(n_out // pair):
                start = n * span
                turned = jnp.dot(
                    turn_ref[n],
                    half[q * rows + start : q * rows + start + span],
                    preferred_element_type=F32,
                )
                o_ref[q, start : start + span, :] = (turned * scale[start : start + span]).astype(
                    BF16
                )

    grid_spec = pltpu.PrefetchScalarGridSpec(
        num_scalar_prefetch=1,
        grid=(tiles,),
        in_specs=[
            pl.BlockSpec((1, queries, rows, cols), lambda b, m: (b, 0, 0, 0)),
            pl.BlockSpec((1, rows, cols), lambda b, m: (b, 0, 0)),
            pl.BlockSpec(sums.shape, lambda b, m: (0, 0)),
            pl.BlockSpec((n_out, width, width), lambda b, m: (m[0] * groups + b // in_tiles, 0, 0)),
            pl.BlockSpec((n_in, width, width), lambda b, m: (b % in_tiles, 0, 0)),
        ]
        + [pl.BlockSpec(memory_space=pl.ANY)] * len(after),
        out_specs=pl.BlockSpec(
            (queries, rows, cols), lambda b, m: (0, b // in_tiles, b % in_tiles)
        ),
        scratch_shapes=[pltpu.VMEM((n_out // pair, span, span), BF16)],
    )
    return call(
        body,
        grid_spec=grid_spec,
        out_shape=jax.ShapeDtypeStruct((queries, groups * rows, features), BF16),
        name="precondition",
        cost=COST_PRE,
    )(me[None], query_grads, eigenvalues, sums, out_basis, in_basis, *after)


def join_and_tally(where, turned_piece, pieces, early, in_basis, own, sibling, starts, ends, order):
    queries, rows, features = own.shape
    docs, tokens = starts.shape
    width = in_basis.shape[1]
    block = math.gcd(rows, 512)
    all_pieces = [turned_piece] + list(pieces)
    count = len(all_pieces)
    raw = [x for x, _ in pieces] + list(early)
    cut = turned_piece[0][0].shape[0]
    raw_place = [next(i for i, o in enumerate(order) if o is x) for x, _ in raw]
    heights = [array.shape[0] for array in order]
    tops = [sum(heights[:i]) for i in range(len(heights))]
    grads = [g for _, (g, _) in all_pieces]
    operands = list(order) + [in_hbm(in_basis), *turned_piece[0]]
    operands += [in_hbm(g) for g in grads] + [own, sibling, starts, ends]

    def body(where_ref, *refs):
        raw_refs = refs[: len(order)]
        basis_hbm, high_hbm, low_hbm = refs[len(order) : len(order) + 3]
        g_hbm = refs[len(order) + 3 : len(order) + 3 + count]
        own_ref, sib_ref, st_ref, en_ref, o_ref, both_ref = refs[
            len(order) + 3 + count : len(operands) + 2
        ]
        t_refs = refs[len(operands) + 2 : -7]
        raw_all, basis_ref, x_all, g_all, x_sems, g_sems, p_sems = refs[-7:]
        x_copies = [pltpu.make_async_copy(basis_hbm, basis_ref, x_sems.at[len(order)])]
        x_copies += [
            pltpu.make_async_copy(
                raw_refs[i], raw_all.at[pl.ds(tops[i], heights[i])], x_sems.at[i]
            )
            for i in range(len(order))
        ]
        copies = [
            [
                pltpu.make_async_copy(p_ref.at[q], both_ref.at[c, q], p_sems.at[c, q])
                for q in range(queries)
            ]
            for c, p_ref in enumerate((own_ref, sib_ref))
        ]
        x_copies += [
            pltpu.make_async_copy(
                high_hbm, x_all.at[pl.ds(0, cut), pl.ds(0, tokens)], x_sems.at[len(order) + 1]
            ),
            pltpu.make_async_copy(
                low_hbm.at[pl.ds(0, features - cut)],
                x_all.at[pl.ds(cut, features - cut), pl.ds(0, tokens)],
                x_sems.at[len(order) + 2],
            ),
        ]
        g_copies = [
            pltpu.make_async_copy(
                g_hbm[n].at[pl.ds(all_pieces[n][1][1], 2 * rows)], g_all.at[n], g_sems.at[n]
            )
            for n in range(count)
        ]
        for copy in x_copies:
            copy.start()
        copies[0][0].start()
        for copy in g_copies:
            copy.start()
        for c in range(2):
            for q in range(queries):
                if c or q:
                    copies[c][q].start()
        for copy in x_copies:
            copy.wait()
        for n, (_, first) in enumerate(raw):
            turn(raw_all, tops[raw_place[n]] + first, tokens, basis_ref, x_all, (n + 1) * tokens)
        scores = [[jnp.zeros((1, tokens), F32)] * queries for _ in all_pieces]
        for c in range(2):
            core = where_ref[0] if c == 0 else 1 - where_ref[0]
            for q in range(queries):
                copies[c][q].wait()
                if c == 0 and q == 0:
                    for copy in g_copies:
                        copy.wait()
                for r in range(0, rows, block):
                    turned = jnp.dot(
                        both_ref[c, q, r : r + block, :], x_all[...], preferred_element_type=F32
                    )
                    for n, t_ref in enumerate(t_refs):
                        left = (count + n) * tokens
                        t_ref[c, q, r : r + block, :] = turned[:, left : left + tokens]
                    for n in range(count):
                        spot = pl.ds(pl.multiple_of(core * rows + r, block), block)
                        scores[n][q] = scores[n][q] + jnp.sum(
                            turned[:, n * tokens : (n + 1) * tokens]
                            * g_all[n, spot, :].astype(F32),
                            axis=0,
                            keepdims=True,
                        )
        add_shares(where_ref, scores, None, st_ref, en_ref, o_ref)

    hbm = pl.BlockSpec(memory_space=pl.ANY)
    vmem = pl.BlockSpec(memory_space=pltpu.VMEM)
    kept = jax.ShapeDtypeStruct((2, queries, rows, tokens), F32)
    return call(
        body,
        in_specs=[pl.BlockSpec(memory_space=pltpu.SMEM)]
        + [hbm] * (len(order) + 3 + count)
        + [hbm, hbm, vmem, vmem],
        out_specs=[vmem] * (2 + len(early)),
        out_shape=[
            jax.ShapeDtypeStruct((queries, docs, tokens), F32),
            jax.ShapeDtypeStruct((2,) + own.shape, own.dtype),
        ]
        + [kept] * len(early),
        scratch_shapes=[
            pltpu.VMEM((sum(heights), features), BF16),
            pltpu.VMEM(in_basis.shape, BF16),
            pltpu.VMEM((features, (count + len(early)) * tokens), BF16),
            pltpu.VMEM((count, 2 * rows, tokens), BF16),
            pltpu.SemaphoreType.DMA((len(order) + 3,)),
            pltpu.SemaphoreType.DMA((count,)),
            pltpu.SemaphoreType.DMA((2, queries)),
        ],
        name="join_and_tally",
    )(where, *operands)


def add_shares(where_ref, scores, run_ref, st_ref, en_ref, o_ref):
    docs, tokens = st_ref.shape
    for q in range(len(scores[0])):
        total = jnp.zeros((docs, tokens), F32) if run_ref is None else run_ref[q]
        for n in range(len(scores)):
            spot = where_ref[1 + n] * tokens + lax.broadcasted_iota(jnp.int32, (docs, tokens), 1)
            inside = (spot >= st_ref[...]) & (spot < en_ref[...])
            total = total + jnp.where(inside, scores[n][q], 0.0)
        o_ref[q] = total


def project(inputs, rows_of, both, after, base=None):
    cores, queries, rows, features = both.shape
    tokens = inputs.shape[1]
    first, end = rows_of
    block = math.gcd(rows, 512)
    bases = [] if base is None else [base]

    def body(x_ref, p_ref, *refs):
        for c in range(cores):
            for q in range(queries):
                for r in range(0, rows, block):
                    span = slice(r, r + block)
                    turned = jnp.dot(
                        p_ref[c, q, span, first:end],
                        x_ref[: end - first, :],
                        preferred_element_type=F32,
                    )
                    refs[-1][c, q, span, :] = refs[0][c, q, span, :] + turned if bases else turned

    vmem = pl.BlockSpec(memory_space=pltpu.VMEM)
    return call(
        body,
        in_specs=[vmem] * (2 + len(bases)) + [pl.BlockSpec(memory_space=pl.ANY)] * len(after),
        out_specs=vmem,
        out_shape=jax.ShapeDtypeStruct((cores, queries, rows, tokens), F32),
        name="project",
    )(inputs, both, *bases, *after)


def tally(where, projected, grads, starts, ends, running, order):
    cores, queries, rows, tokens = projected[0].shape
    block = math.gcd(rows, 512)
    arrays = list(order)
    places = [next(i for i, o in enumerate(arrays) if o is array) for array, _ in grads]
    held = len(projected)

    def body(where_ref, *refs):
        g_refs = refs[held : held + len(arrays)]
        st_ref, en_ref, run_ref, o_ref = refs[held + len(arrays) :]
        scores = [[jnp.zeros((1, tokens), F32)] * queries for _ in grads]
        for c in range(cores):
            core = where_ref[0] if c == 0 else 1 - where_ref[0]
            for q in range(queries):
                for r in range(0, rows, block):
                    for n, (_, first) in enumerate(grads):
                        spot = pl.ds(pl.multiple_of(core * rows + first + r, block), block)
                        scores[n][q] = scores[n][q] + jnp.sum(
                            refs[n][c, q, r : r + block, :]
                            * g_refs[places[n]][spot, :].astype(F32),
                            axis=0,
                            keepdims=True,
                        )
        add_shares(where_ref, scores, run_ref, st_ref, en_ref, o_ref)

    vmem = pl.BlockSpec(memory_space=pltpu.VMEM)
    return call(
        body,
        in_specs=[pl.BlockSpec(memory_space=pltpu.SMEM)] + [vmem] * (held + len(arrays) + 3),
        out_specs=vmem,
        out_shape=jax.ShapeDtypeStruct(running.shape, F32),
        name="tally",
    )(where, *projected, *arrays, starts, ends, running)


def local_rows(
    depth, layer_inputs, output_grads, query_grads, eigenvalues, out_basis, in_basis, doc_lengths
):
    devices = 4 * depth
    chips = 2 * depth
    tokens = layer_inputs.shape[0]
    queries = query_grads.shape[1]
    entries = output_grads.shape[1] * layer_inputs.shape[1]
    me = lax.axis_index("dp")
    chip = me // 2
    core = me % 2

    def swap(value, offset):
        return lax.ppermute(value, "dp", [(i, i ^ offset) for i in range(devices)])

    features = layer_inputs.shape[1]
    part = output_grads.shape[1] // chips
    spin = functools.partial(rotate, output_grads, out_basis, chip, chips)
    far_x = swap(layer_inputs, 12)
    near_x = swap(layer_inputs, 4)
    side_x = swap(layer_inputs, 2)
    sums = sum_eigenvalues(eigenvalues)
    (side_g,) = spin([[1, 3, 7]], [sums], cost=COST_K1)
    side_g = swap(side_g, 2)

    g_own, middle, g_far, near_g = spin([[0], [4, 5], [6], [2]], cost=COST_KG)
    sums = sums + swap(sums, 2)
    sums = hold(sums, middle)
    for offset in (1, 4):
        sums = sums + swap(sums, offset)

    sides_sent, middle = pair_up(near_x, far_x, middle, [side_x])
    middle = swap(middle, 8)
    middle_x = swap(far_x, 4)
    sides = swap(sides_sent, 2)

    sums = hold(sums, sides_sent)
    sums = sums + swap(sums, 8)
    own = precondition_rows(
        query_grads, eigenvalues, sums, out_basis, in_basis, me, entries, [near_x, far_x, side_x, side_g]
    )
    sibling = swap(own, 1)

    near_g, g_far = pack_grads(near_g, g_far, side_g)
    near_g = swap(near_g, 4)
    g_far = swap(g_far, 12)
    cut = features * 3 // 4
    turned = last_round(middle_x, middle, in_basis, cut, [sides, own])
    high, low = [swap(value, 2) for value in turned]

    doc_ends = jnp.cumsum(doc_lengths)
    doc_starts = doc_ends - doc_lengths
    docs = doc_lengths.shape[0]
    starts = jnp.broadcast_to(doc_starts[:, None], (docs, tokens))
    ends = jnp.broadcast_to(doc_ends[:, None], (docs, tokens))

    def where(*offsets):
        return jnp.stack([core] + [me ^ (2 * k) for k in offsets]).astype(jnp.int32)

    layer_inputs = in_hbm(layer_inputs)
    running, both, *kept = join_and_tally(
        where(4, 0, 1),
        (turned, (middle, 0)),
        [((layer_inputs, 0), (g_own, 0)), ((side_x, 0), (side_g, 0))],
        [(near_x, 0), (sides, 0), (far_x, 0), (sides, tokens)],
        in_basis,
        own,
        sibling,
        starts,
        ends,
        [layer_inputs, side_x, near_x, far_x, sides],
    )
    part_way = project(high, (0, cut), both, [running])
    kept.append(project(low, (cut, features), both, [], part_way))
    running = tally(
        where(2, 3, 6, 7, 5),
        kept,
        [(near_g, 0), (near_g, part), (g_far, 0), (g_far, part), (low, features - cut)],
        starts,
        ends,
        running,
        [near_g, g_far, low],
    )
    shares = jnp.sum(running, axis=2)
    for offset in (1, 2, 4, 8):
        shares = shares + swap(shares, offset)
    each = docs // devices
    mine = lax.dynamic_slice_in_dim(shares, me * each, each, 1)
    return mine.T


def local(layer_inputs, output_grads, query_grads, eigenvalues, out_basis, in_basis, doc_lengths, devices):
    args = (layer_inputs, output_grads, query_grads, eigenvalues, out_basis, in_basis, doc_lengths)
    in_tiles = layer_inputs.shape[1] // query_grads.shape[3]
    tile_count = query_grads.shape[0]
    if devices == 16 and tile_count % in_tiles == 0:
        return local_rows(devices // 4, *args)
    return local_general(*args)


def solution(mesh):
    in_specs = (
        P(("groups", "dp"), None),
        P(("groups", "dp"), None),
        P("dp", None, None, None),
        P("dp", None, None),
        P(),
        P(),
        P("groups"),
    )
    out_specs = P(("groups", "dp"), None)
    body = functools.partial(local, devices=mesh.shape["dp"])
    return jax.shard_map(body, mesh=mesh, in_specs=in_specs, out_specs=out_specs, check_vma=False)
```

```python
import functools
import math

import jax
import jax.numpy as jnp
from jax import lax
from jax.experimental import pallas as pl
from jax.experimental.pallas import tpu as pltpu
from jax.sharding import PartitionSpec as P

VMEM_LIMIT = 16 * 1024 * 1024
COST_PRE = 10**11
COST_K1 = 1
COST_KG = 10**11
COST_K3 = 10**11
F32 = jnp.float32
BF16 = jnp.bfloat16


def turn_rows(columns, basis_blocks):
    group_count = basis_blocks.shape[0]
    block_width = basis_blocks.shape[1]
    grouped = columns.reshape(columns.shape[0], group_count, block_width)
    turned = jnp.einsum("tnk,nkj->tnj", grouped, basis_blocks, preferred_element_type=jnp.float32)
    return turned.reshape(columns.shape).astype(jnp.bfloat16)


def precondition(query_grads, eigenvalues, damping, tile_out, tile_in):
    blocks, queries, rows_out, rows_in = query_grads.shape
    block_width = tile_in.shape[-1]
    grouped = query_grads.reshape(blocks, queries, rows_out, rows_in // block_width, block_width)
    half_turned = jnp.einsum(
        "bqonk,bnkj->bqonj", grouped, tile_in, preferred_element_type=jnp.float32
    )
    half_turned = half_turned.reshape(blocks, queries, rows_out, rows_in).astype(jnp.bfloat16)
    grouped = half_turned.reshape(blocks, queries, rows_out // block_width, block_width, rows_in)
    turned = jnp.einsum("bqnki,bnkj->bqnji", grouped, tile_out, preferred_element_type=jnp.float32)
    turned = turned.reshape(blocks, queries, rows_out, rows_in)
    return (turned / (eigenvalues[:, None] + damping)).astype(jnp.bfloat16)


def tally_scores(grads_got, inputs_got, preconditioned, doc_starts, doc_ends):
    blocks, total_rows, rows_out = grads_got.shape
    queries = preconditioned.shape[1]
    row_step = math.gcd(1024, total_rows)
    flat_pre = preconditioned.reshape(blocks, queries * rows_out, preconditioned.shape[3])

    def one_piece(running, piece_index):
        start_row = piece_index * row_step
        grads_piece = lax.dynamic_slice_in_dim(grads_got, start_row, row_step, 1)
        inputs_piece = lax.dynamic_slice_in_dim(inputs_got, start_row, row_step, 1)
        projected = jnp.einsum(
            "bti,bpi->btp", inputs_piece, flat_pre, preferred_element_type=jnp.float32
        )
        projected = projected.reshape(blocks, row_step, queries, rows_out)
        scores = jnp.sum(projected * grads_piece[:, :, None, :].astype(jnp.float32), axis=(0, 3))
        positions = start_row + lax.iota(jnp.int32, row_step)
        member = (
            (positions[:, None] >= doc_starts[None, :]) & (positions[:, None] < doc_ends[None, :])
        ).astype(jnp.float32)
        added = jnp.einsum("td,tq->dq", member, scores, precision=lax.Precision.HIGHEST)
        return (running + added, None)

    initial = jnp.zeros((doc_starts.shape[0], queries), jnp.float32)
    summed, _ = lax.scan(one_piece, initial, jnp.arange(total_rows // row_step, dtype=jnp.int32))
    return summed


def local_general(
    layer_inputs, output_grads, query_grads, eigenvalues, out_basis, in_basis, doc_lengths
):
    block_width = out_basis.shape[1]
    tok_count = layer_inputs.shape[0]
    tile_count = query_grads.shape[0]
    rows_out = query_grads.shape[2]
    rows_in = query_grads.shape[3]
    in_tiles = layer_inputs.shape[1] // rows_in
    out_tiles = output_grads.shape[1] // rows_out
    tile_ids = lax.axis_index("dp") * tile_count + lax.iota(jnp.int32, tile_count)
    out_sets = out_basis.reshape(out_tiles, rows_out // block_width, block_width, block_width)
    in_sets = in_basis.reshape(in_tiles, rows_in // block_width, block_width, block_width)
    tile_out = jnp.take(out_sets, tile_ids // in_tiles, axis=0)
    tile_in = jnp.take(in_sets, tile_ids % in_tiles, axis=0)
    eigen_sum = lax.psum(jnp.sum(eigenvalues), "dp")
    entries = output_grads.shape[1] * layer_inputs.shape[1]
    damping = 0.1 * (eigen_sum / entries)
    preconditioned = precondition(query_grads, eigenvalues, damping, tile_out, tile_in)
    grads_local = turn_rows(output_grads, out_basis)
    inputs_local = turn_rows(layer_inputs, in_basis)
    grads_tiles = grads_local.reshape(tok_count, out_tiles, rows_out).transpose(1, 0, 2)[:, None]
    grads_tiles = jnp.broadcast_to(grads_tiles, (out_tiles, in_tiles, tok_count, rows_out))
    grads_tiles = grads_tiles.reshape(out_tiles * in_tiles, tok_count, rows_out)
    inputs_tiles = inputs_local.reshape(tok_count, in_tiles, rows_in).transpose(1, 0, 2)[None]
    inputs_tiles = jnp.broadcast_to(inputs_tiles, (out_tiles, in_tiles, tok_count, rows_in))
    inputs_tiles = inputs_tiles.reshape(out_tiles * in_tiles, tok_count, rows_in)
    grads_got, inputs_got = (
        lax.all_to_all(grads_tiles, "dp", split_axis=0, concat_axis=1, tiled=True),
        lax.all_to_all(inputs_tiles, "dp", split_axis=0, concat_axis=1, tiled=True),
    )
    doc_ends = jnp.cumsum(doc_lengths)
    doc_starts = doc_ends - doc_lengths
    partial_scores = tally_scores(grads_got, inputs_got, preconditioned, doc_starts, doc_ends)
    return lax.psum_scatter(partial_scores, "dp", scatter_dimension=0, tiled=True)


def dot_tt(a, b):
    return lax.dot_general(a, b, (((0,), (1,)), ((), ())), preferred_element_type=F32)


def call(body, cost=1, **kw):
    return pl.pallas_call(
        body,
        compiler_params=pltpu.CompilerParams(vmem_limit_bytes=VMEM_LIMIT),
        cost_estimate=pl.CostEstimate(flops=cost, bytes_accessed=1, transcendentals=0),
        **kw,
    )


def in_hbm(value):
    return pltpu.with_memory_space_constraint(value, pltpu.HBM)


def rotate(output_grads, out_basis, chip, chips, layouts, after=(), cost=1):
    tokens, units = output_grads.shape
    width = out_basis.shape[1]
    part = units // chips
    per = part // width
    offsets = [k for layout in layouts for k in layout]
    count = len(offsets)

    def body(chip_ref, g_hbm, b_hbm, *refs):
        o_refs = refs[len(after) : len(after) + len(layouts)]
        g_all, b_all, g_sems, b_sems = refs[len(after) + len(layouts) :]
        copies = []
        for n, k in enumerate(offsets):
            place = chip_ref[0] ^ k
            cols = pl.ds(pl.multiple_of(place * part, part), part)
            blocks = pl.ds(place * per, per)
            copies.append(
                (
                    pltpu.make_async_copy(g_hbm.at[:, cols], g_all.at[n], g_sems.at[n]),
                    pltpu.make_async_copy(b_hbm.at[blocks], b_all.at[n], b_sems.at[n]),
                )
            )
        for pair in copies:
            for copy in pair:
                copy.start()
        n = 0
        for o_ref, layout in zip(o_refs, layouts):
            for top in range(len(layout)):
                for copy in copies[n]:
                    copy.wait()
                for i in range(per):
                    span = slice(i * width, (i + 1) * width)
                    first = top * part + i * width
                    turned = jnp.dot(g_all[n, :, span], b_all[n, i], preferred_element_type=F32)
                    o_ref[first : first + width, :] = turned.astype(BF16).T
                n += 1

    hbm = pl.BlockSpec(memory_space=pl.ANY)
    vmem = pl.BlockSpec(memory_space=pltpu.VMEM)
    return call(
        body,
        cost=cost,
        in_specs=[pl.BlockSpec(memory_space=pltpu.SMEM), hbm, hbm] + [hbm] * len(after),
        out_specs=[vmem] * len(layouts),
        out_shape=[jax.ShapeDtypeStruct((part * len(l), tokens), BF16) for l in layouts],
        scratch_shapes=[
            pltpu.VMEM((count, tokens, part), BF16),
            pltpu.VMEM((count, per, width, width), BF16),
            pltpu.SemaphoreType.DMA((count,)),
            pltpu.SemaphoreType.DMA((count,)),
        ],
        name="rotate",
    )(chip[None], in_hbm(output_grads), in_hbm(out_basis), *after)


def turn(x_ref, first, tokens, basis_ref, o_ref, left=0, cut=None, rest_ref=None):
    count, width, _ = basis_ref.shape
    for i in range(count):
        span = slice(i * width, (i + 1) * width)
        turned = jnp.dot(
            x_ref[first : first + tokens, span], basis_ref[i], preferred_element_type=F32
        )
        turned = turned.astype(BF16).T
        if cut is None or i * width < cut:
            o_ref[span, left : left + tokens] = turned
        else:
            rest_ref[i * width - cut : (i + 1) * width - cut, :] = turned


def turn_inputs(arrays, in_basis):
    count, width, _ = in_basis.shape
    tokens = arrays[0].shape[0]

    def body(*refs):
        for n in range(len(arrays)):
            turn(refs[n], 0, tokens, refs[len(arrays)], refs[len(arrays) + 1 + n])

    vmem = pl.BlockSpec(memory_space=pltpu.VMEM)
    return call(
        body,
        in_specs=[vmem] * (len(arrays) + 1),
        out_specs=[vmem] * len(arrays),
        out_shape=[jax.ShapeDtypeStruct((count * width, tokens), BF16)] * len(arrays),
        name="turn_inputs",
    )(*arrays, in_basis)


def pair_up(a, b, held, after):
    def body(a_ref, b_ref, *refs):
        o_ref = refs[1 + len(after)]
        o_ref[: a.shape[0], :] = a_ref[...]
        o_ref[a.shape[0] :, :] = b_ref[...]

    anywhere = pl.BlockSpec(memory_space=pl.ANY)
    vmem = pl.BlockSpec(memory_space=pltpu.VMEM)
    return call(
        body,
        in_specs=[vmem, vmem] + [anywhere] * (1 + len(after)),
        out_specs=[vmem, anywhere],
        out_shape=[
            jax.ShapeDtypeStruct((a.shape[0] + b.shape[0], a.shape[1]), a.dtype),
            jax.ShapeDtypeStruct(held.shape, held.dtype),
        ],
        input_output_aliases={2: 1},
        name="pair_up",
    )(a, b, held, *after)


def pack_grads(near, far, across):
    part, tokens = near.shape

    def body(n_ref, f_ref, a_ref, near_ref, far_ref, sems):
        top, low = pl.ds(0, part), pl.ds(part, part)
        copies = [
            pltpu.make_async_copy(n_ref, near_ref.at[top], sems.at[0]),
            pltpu.make_async_copy(a_ref.at[low], near_ref.at[low], sems.at[1]),
            pltpu.make_async_copy(f_ref, far_ref.at[top], sems.at[2]),
            pltpu.make_async_copy(a_ref.at[pl.ds(2 * part, part)], far_ref.at[low], sems.at[3]),
        ]
        for copy in copies:
            copy.start()
        for copy in copies:
            copy.wait()

    anywhere = pl.BlockSpec(memory_space=pl.ANY)
    vmem = pl.BlockSpec(memory_space=pltpu.VMEM)
    return call(
        body,
        in_specs=[anywhere] * 3,
        out_specs=[vmem] * 2,
        out_shape=[jax.ShapeDtypeStruct((2 * part, tokens), BF16)] * 2,
        scratch_shapes=[pltpu.SemaphoreType.DMA((4,))],
        name="pack_grads",
    )(near, far, across)


def last_round(x, middle, in_basis, cut, after):
    tokens = x.shape[0]
    count, width, _ = in_basis.shape
    features = count * width
    part = middle.shape[0] // 2

    def body(x_ref, m_ref, b_ref, *refs):
        high_ref, low_ref, sem = refs[len(after) :]
        copy = pltpu.make_async_copy(
            m_ref.at[pl.ds(part, part)], low_ref.at[pl.ds(features - cut, part)], sem
        )
        copy.start()
        turn(x_ref, 0, tokens, b_ref, high_ref, 0, cut, low_ref)
        copy.wait()

    anywhere = pl.BlockSpec(memory_space=pl.ANY)
    vmem = pl.BlockSpec(memory_space=pltpu.VMEM)
    return call(
        body,
        cost=COST_K3,
        in_specs=[vmem, anywhere, vmem] + [anywhere] * len(after),
        out_specs=[vmem] * 2,
        out_shape=[
            jax.ShapeDtypeStruct((cut, tokens), BF16),
            jax.ShapeDtypeStruct((features - cut + part, tokens), BF16),
        ],
        scratch_shapes=[pltpu.SemaphoreType.DMA],
        name="last_round",
    )(x, middle, in_basis, *after)


def sum_eigenvalues(eigenvalues):
    tiles, rows, cols = eigenvalues.shape

    def body(e_ref, o_ref):
        @pl.when(pl.program_id(0) == 0)
        def _():
            o_ref[...] = jnp.zeros_like(o_ref)

        part = jnp.sum(e_ref[0].reshape(rows // 8, 8, cols), axis=0)
        total = part[:, :128]
        for n in range(1, cols // 128):
            total = total + part[:, n * 128 : (n + 1) * 128]
        o_ref[...] += total

    return call(
        body,
        grid=(tiles,),
        in_specs=[pl.BlockSpec((1, rows, cols), lambda b: (b, 0, 0))],
        out_specs=pl.BlockSpec((8, 128), lambda b: (0, 0)),
        out_shape=jax.ShapeDtypeStruct((8, 128), F32),
        name="sum_eigenvalues",
    )(eigenvalues)


def hold(value, *after):
    def body(v_ref, *refs):
        refs[-1][...] = v_ref[...]

    vmem = pl.BlockSpec(memory_space=pltpu.VMEM)
    return call(
        body,
        in_specs=[vmem] + [pl.BlockSpec(memory_space=pl.ANY)] * len(after),
        out_specs=vmem,
        out_shape=jax.ShapeDtypeStruct(value.shape, value.dtype),
        name="hold",
    )(value, *after)


def block_diagonal(blocks):
    count, width = len(blocks), blocks[0].shape[0]
    zero = jnp.zeros((width, width), blocks[0].dtype)
    rows = [
        jnp.concatenate([blocks[i] if i == j else zero for j in range(count)], axis=1)
        for i in range(count)
    ]
    return jnp.concatenate(rows, axis=0)


def precondition_rows(query_grads, eigenvalues, sums, out_basis, in_basis, me, entries, after):
    tiles, queries, rows, cols = query_grads.shape
    width = in_basis.shape[1]
    features = in_basis.shape[0] * width
    in_tiles = features // cols
    groups = tiles // in_tiles
    n_out, n_in = rows // width, cols // width
    pair = 2 if n_out % 2 == 0 else 1
    span = pair * width

    def body(me_ref, q_ref, e_ref, s_ref, ob_ref, ib_ref, *refs):
        o_ref, turn_ref = refs[len(after) :]

        @pl.when(pl.program_id(0) % in_tiles == 0)
        def _():
            for n in range(n_out // pair):
                turn_ref[n] = block_diagonal([ob_ref[n * pair + k].T for k in range(pair)])

        damping = 0.1 * (jnp.sum(s_ref[...], keepdims=True) / entries)
        scale = 1.0 / (e_ref[0] + damping)
        half = jnp.dot(
            q_ref[0].reshape(queries * rows, cols),
            block_diagonal([ib_ref[n] for n in range(n_in)]),
            preferred_element_type=F32,
        ).astype(BF16)
        for q in range(queries):
            for n in range(n_out // pair):
                start = n * span
                turned = jnp.dot(
                    turn_ref[n],
                    half[q * rows + start : q * rows + start + span],
                    preferred_element_type=F32,
                )
                o_ref[q, start : start + span, :] = (turned * scale[start : start + span]).astype(
                    BF16
                )

    grid_spec = pltpu.PrefetchScalarGridSpec(
        num_scalar_prefetch=1,
        grid=(tiles,),
        in_specs=[
            pl.BlockSpec((1, queries, rows, cols), lambda b, m: (b, 0, 0, 0)),
            pl.BlockSpec((1, rows, cols), lambda b, m: (b, 0, 0)),
            pl.BlockSpec(sums.shape, lambda b, m: (0, 0)),
            pl.BlockSpec((n_out, width, width), lambda b, m: (m[0] * groups + b // in_tiles, 0, 0)),
            pl.BlockSpec((n_in, width, width), lambda b, m: (b % in_tiles, 0, 0)),
        ]
        + [pl.BlockSpec(memory_space=pl.ANY)] * len(after),
        out_specs=pl.BlockSpec(
            (queries, rows, cols), lambda b, m: (0, b // in_tiles, b % in_tiles)
        ),
        scratch_shapes=[pltpu.VMEM((n_out // pair, span, span), BF16)],
    )
    return call(
        body,
        grid_spec=grid_spec,
        out_shape=jax.ShapeDtypeStruct((queries, groups * rows, features), BF16),
        name="precondition",
        cost=COST_PRE,
    )(me[None], query_grads, eigenvalues, sums, out_basis, in_basis, *after)


def join_and_tally(where, turned_piece, pieces, early, in_basis, own, sibling, starts, ends, order):
    queries, rows, features = own.shape
    docs, tokens = starts.shape
    width = in_basis.shape[1]
    block = math.gcd(rows, 512)
    all_pieces = [turned_piece] + list(pieces)
    count = len(all_pieces)
    raw = [x for x, _ in pieces] + list(early)
    ready = [x.shape[0] == features for x, _ in raw]
    cut = turned_piece[0][0].shape[0]
    raw_place = [next(i for i, o in enumerate(order) if o is x) for x, _ in raw]
    heights = [0 if a.shape[0] == features else a.shape[0] for a in order]
    tops = [sum(heights[:i]) for i in range(len(heights))]
    grads = [g for _, (g, _) in all_pieces]
    operands = [in_hbm(a) for a in order] + [in_hbm(in_basis), *turned_piece[0]]
    operands += [in_hbm(g) for g in grads] + [own, sibling, starts, ends]

    def body(where_ref, *refs):
        raw_refs = refs[: len(order)]
        basis_hbm, high_hbm, low_hbm = refs[len(order) : len(order) + 3]
        g_hbm = refs[len(order) + 3 : len(order) + 3 + count]
        own_ref, sib_ref, st_ref, en_ref, o_ref, both_ref = refs[
            len(order) + 3 + count : len(operands) + 2
        ]
        t_refs = refs[len(operands) + 2 : -7]
        raw_all, basis_ref, x_all, g_all, x_sems, g_sems, p_sems = refs[-7:]
        x_copies = [pltpu.make_async_copy(basis_hbm, basis_ref, x_sems.at[len(order)])]
        for n, i in enumerate(raw_place):
            if ready[n]:
                place = x_all.at[:, pl.ds((n + 1) * tokens, tokens)]
                x_copies.append(pltpu.make_async_copy(raw_refs[i], place, x_sems.at[i]))
        for i in range(len(order)):
            if heights[i]:
                place = raw_all.at[pl.ds(tops[i], heights[i])]
                x_copies.append(pltpu.make_async_copy(raw_refs[i], place, x_sems.at[i]))
        copies = [
            [
                pltpu.make_async_copy(p_ref.at[q], both_ref.at[c, q], p_sems.at[c, q])
                for q in range(queries)
            ]
            for c, p_ref in enumerate((own_ref, sib_ref))
        ]
        x_copies += [
            pltpu.make_async_copy(
                high_hbm, x_all.at[pl.ds(0, cut), pl.ds(0, tokens)], x_sems.at[len(order) + 1]
            ),
            pltpu.make_async_copy(
                low_hbm.at[pl.ds(0, features - cut)],
                x_all.at[pl.ds(cut, features - cut), pl.ds(0, tokens)],
                x_sems.at[len(order) + 2],
            ),
        ]
        g_copies = [
            pltpu.make_async_copy(
                g_hbm[n].at[pl.ds(all_pieces[n][1][1], 2 * rows)], g_all.at[n], g_sems.at[n]
            )
            for n in range(count)
        ]
        for copy in x_copies:
            copy.start()
        copies[0][0].start()
        for copy in g_copies:
            copy.start()
        for c in range(2):
            for q in range(queries):
                if c or q:
                    copies[c][q].start()
        for copy in x_copies:
            copy.wait()
        for n, (_, first) in enumerate(raw):
            if ready[n]:
                continue
            turn(raw_all, tops[raw_place[n]] + first, tokens, basis_ref, x_all, (n + 1) * tokens)
        scores = [[jnp.zeros((1, tokens), F32)] * queries for _ in all_pieces]
        for c in range(2):
            core = where_ref[0] if c == 0 else 1 - where_ref[0]
            for q in range(queries):
                copies[c][q].wait()
                if c == 0 and q == 0:
                    for copy in g_copies:
                        copy.wait()
                for r in range(0, rows, block):
                    turned = jnp.dot(
                        both_ref[c, q, r : r + block, :], x_all[...], preferred_element_type=F32
                    )
                    for n, t_ref in enumerate(t_refs):
                        left = (count + n) * tokens
                        t_ref[c, q, r : r + block, :] = turned[:, left : left + tokens]
                    for n in range(count):
                        spot = pl.ds(pl.multiple_of(core * rows + r, block), block)
                        scores[n][q] = scores[n][q] + jnp.sum(
                            turned[:, n * tokens : (n + 1) * tokens]
                            * g_all[n, spot, :].astype(F32),
                            axis=0,
                            keepdims=True,
                        )
        add_shares(where_ref, scores, None, st_ref, en_ref, o_ref)

    hbm = pl.BlockSpec(memory_space=pl.ANY)
    vmem = pl.BlockSpec(memory_space=pltpu.VMEM)
    kept = jax.ShapeDtypeStruct((2, queries, rows, tokens), F32)
    return call(
        body,
        in_specs=[pl.BlockSpec(memory_space=pltpu.SMEM)]
        + [hbm] * (len(order) + 3 + count)
        + [hbm, hbm, vmem, vmem],
        out_specs=[vmem] * (2 + len(early)),
        out_shape=[
            jax.ShapeDtypeStruct((queries, docs, tokens), F32),
            jax.ShapeDtypeStruct((2,) + own.shape, own.dtype),
        ]
        + [kept] * len(early),
        scratch_shapes=[
            pltpu.VMEM((sum(heights), features), BF16),
            pltpu.VMEM(in_basis.shape, BF16),
            pltpu.VMEM((features, (count + len(early)) * tokens), BF16),
            pltpu.VMEM((count, 2 * rows, tokens), BF16),
            pltpu.SemaphoreType.DMA((len(order) + 3,)),
            pltpu.SemaphoreType.DMA((count,)),
            pltpu.SemaphoreType.DMA((2, queries)),
        ],
        name="join_and_tally",
    )(where, *operands)


def add_shares(where_ref, scores, run_ref, st_ref, en_ref, o_ref):
    docs, tokens = st_ref.shape
    for q in range(len(scores[0])):
        total = jnp.zeros((docs, tokens), F32) if run_ref is None else run_ref[q]
        for n in range(len(scores)):
            spot = where_ref[1 + n] * tokens + lax.broadcasted_iota(jnp.int32, (docs, tokens), 1)
            inside = (spot >= st_ref[...]) & (spot < en_ref[...])
            total = total + jnp.where(inside, scores[n][q], 0.0)
        o_ref[q] = total


def project(inputs, rows_of, both, after, base=None):
    cores, queries, rows, features = both.shape
    tokens = inputs.shape[1]
    first, end = rows_of
    block = math.gcd(rows, 512)
    bases = [] if base is None else [base]

    def body(x_ref, p_ref, *refs):
        for c in range(cores):
            for q in range(queries):
                for r in range(0, rows, block):
                    span = slice(r, r + block)
                    turned = jnp.dot(
                        p_ref[c, q, span, first:end],
                        x_ref[: end - first, :],
                        preferred_element_type=F32,
                    )
                    refs[-1][c, q, span, :] = refs[0][c, q, span, :] + turned if bases else turned

    vmem = pl.BlockSpec(memory_space=pltpu.VMEM)
    return call(
        body,
        in_specs=[vmem] * (2 + len(bases)) + [pl.BlockSpec(memory_space=pl.ANY)] * len(after),
        out_specs=vmem,
        out_shape=jax.ShapeDtypeStruct((cores, queries, rows, tokens), F32),
        name="project",
    )(inputs, both, *bases, *after)


def tally(where, projected, grads, starts, ends, running, order):
    cores, queries, rows, tokens = projected[0].shape
    block = math.gcd(rows, 512)
    arrays = list(order)
    places = [next(i for i, o in enumerate(arrays) if o is array) for array, _ in grads]
    held = len(projected)

    def body(where_ref, *refs):
        g_refs = refs[held : held + len(arrays)]
        st_ref, en_ref, run_ref, o_ref = refs[held + len(arrays) :]
        scores = [[jnp.zeros((1, tokens), F32)] * queries for _ in grads]
        for c in range(cores):
            core = where_ref[0] if c == 0 else 1 - where_ref[0]
            for q in range(queries):
                for r in range(0, rows, block):
                    for n, (_, first) in enumerate(grads):
                        spot = pl.ds(pl.multiple_of(core * rows + first + r, block), block)
                        scores[n][q] = scores[n][q] + jnp.sum(
                            refs[n][c, q, r : r + block, :]
                            * g_refs[places[n]][spot, :].astype(F32),
                            axis=0,
                            keepdims=True,
                        )
        add_shares(where_ref, scores, run_ref, st_ref, en_ref, o_ref)

    vmem = pl.BlockSpec(memory_space=pltpu.VMEM)
    return call(
        body,
        in_specs=[pl.BlockSpec(memory_space=pltpu.SMEM)] + [vmem] * (held + len(arrays) + 3),
        out_specs=vmem,
        out_shape=jax.ShapeDtypeStruct(running.shape, F32),
        name="tally",
    )(where, *projected, *arrays, starts, ends, running)


def local_rows(
    depth, layer_inputs, output_grads, query_grads, eigenvalues, out_basis, in_basis, doc_lengths
):
    devices = 4 * depth
    chips = 2 * depth
    tokens = layer_inputs.shape[0]
    queries = query_grads.shape[1]
    entries = output_grads.shape[1] * layer_inputs.shape[1]
    me = lax.axis_index("dp")
    chip = me // 2
    core = me % 2

    def swap(value, offset):
        return lax.ppermute(value, "dp", [(i, i ^ offset) for i in range(devices)])

    features = layer_inputs.shape[1]
    part = output_grads.shape[1] // chips
    spin = functools.partial(rotate, output_grads, out_basis, chip, chips)
    far_x = swap(layer_inputs, 12)
    near_x = swap(layer_inputs, 4)
    side_x = swap(layer_inputs, 2)
    sums = sum_eigenvalues(eigenvalues)
    (side_g,) = spin([[1, 3, 7]], [sums], cost=COST_K1)
    side_g = swap(side_g, 2)

    g_own, middle, g_far, near_g = spin([[0], [4, 5], [6], [2]], cost=COST_KG)
    sums = sums + swap(sums, 2)
    sums = hold(sums, middle)
    for offset in (1, 4):
        sums = sums + swap(sums, offset)

    sides_sent, middle = pair_up(near_x, far_x, middle, [side_x])
    middle = swap(middle, 8)
    middle_x = swap(far_x, 4)
    sides = swap(sides_sent, 2)

    sums = hold(sums, sides_sent)
    sums = sums + swap(sums, 8)
    own = precondition_rows(
        query_grads, eigenvalues, sums, out_basis, in_basis, me, entries, [near_x, far_x, side_x, side_g]
    )
    sibling = swap(own, 1)

    near_g, g_far = pack_grads(near_g, g_far, side_g)
    near_g = swap(near_g, 4)
    g_far = swap(g_far, 12)
    cut = features * 3 // 4
    x0, x1, x2, x6 = turn_inputs([layer_inputs, side_x, near_x, far_x], in_basis)
    turned = last_round(middle_x, middle, in_basis, cut, [sides, own, x0])
    high, low = [swap(value, 2) for value in turned]

    doc_ends = jnp.cumsum(doc_lengths)
    doc_starts = doc_ends - doc_lengths
    docs = doc_lengths.shape[0]
    starts = jnp.broadcast_to(doc_starts[:, None], (docs, tokens))
    ends = jnp.broadcast_to(doc_ends[:, None], (docs, tokens))

    def where(*offsets):
        return jnp.stack([core] + [me ^ (2 * k) for k in offsets]).astype(jnp.int32)

    running, both, *kept = join_and_tally(
        where(4, 0, 1),
        (turned, (middle, 0)),
        [((x0, 0), (g_own, 0)), ((x1, 0), (side_g, 0))],
        [(x2, 0), (sides, 0), (x6, 0), (sides, tokens)],
        in_basis,
        own,
        sibling,
        starts,
        ends,
        [x0, x1, x2, x6, sides],
    )
    part_way = project(high, (0, cut), both, [running])
    kept.append(project(low, (cut, features), both, [], part_way))
    running = tally(
        where(2, 3, 6, 7, 5),
        kept,
        [(near_g, 0), (near_g, part), (g_far, 0), (g_far, part), (low, features - cut)],
        starts,
        ends,
        running,
        [near_g, g_far, low],
    )
    shares = jnp.sum(running, axis=2)
    for offset in (1, 2, 4, 8):
        shares = shares + swap(shares, offset)
    each = docs // devices
    mine = lax.dynamic_slice_in_dim(shares, me * each, each, 1)
    return mine.T


def local(layer_inputs, output_grads, query_grads, eigenvalues, out_basis, in_basis, doc_lengths, devices):
    args = (layer_inputs, output_grads, query_grads, eigenvalues, out_basis, in_basis, doc_lengths)
    in_tiles = layer_inputs.shape[1] // query_grads.shape[3]
    tile_count = query_grads.shape[0]
    if devices == 16 and tile_count % in_tiles == 0:
        return local_rows(devices // 4, *args)
    return local_general(*args)


def solution(mesh):
    in_specs = (
        P(("groups", "dp"), None),
        P(("groups", "dp"), None),
        P("dp", None, None, None),
        P("dp", None, None),
        P(),
        P(),
        P("groups"),
    )
    out_specs = P(("groups", "dp"), None)
    body = functools.partial(local, devices=mesh.shape["dp"])
    return jax.shard_map(body, mesh=mesh, in_specs=in_specs, out_specs=out_specs, check_vma=False)
```

```python
import functools
import math

import jax
import jax.numpy as jnp
from jax import lax
from jax.experimental import pallas as pl
from jax.experimental.pallas import tpu as pltpu
from jax.sharding import PartitionSpec as P

VMEM_LIMIT = 16 * 1024 * 1024
COST_PRE = 10**11
COST_K1 = 1
COST_KG = 10**11
COST_K3 = 10**11
F32 = jnp.float32
BF16 = jnp.bfloat16


def turn_rows(columns, basis_blocks):
    group_count = basis_blocks.shape[0]
    block_width = basis_blocks.shape[1]
    grouped = columns.reshape(columns.shape[0], group_count, block_width)
    turned = jnp.einsum("tnk,nkj->tnj", grouped, basis_blocks, preferred_element_type=jnp.float32)
    return turned.reshape(columns.shape).astype(jnp.bfloat16)


def precondition(query_grads, eigenvalues, damping, tile_out, tile_in):
    blocks, queries, rows_out, rows_in = query_grads.shape
    block_width = tile_in.shape[-1]
    grouped = query_grads.reshape(blocks, queries, rows_out, rows_in // block_width, block_width)
    half_turned = jnp.einsum(
        "bqonk,bnkj->bqonj", grouped, tile_in, preferred_element_type=jnp.float32
    )
    half_turned = half_turned.reshape(blocks, queries, rows_out, rows_in).astype(jnp.bfloat16)
    grouped = half_turned.reshape(blocks, queries, rows_out // block_width, block_width, rows_in)
    turned = jnp.einsum("bqnki,bnkj->bqnji", grouped, tile_out, preferred_element_type=jnp.float32)
    turned = turned.reshape(blocks, queries, rows_out, rows_in)
    return (turned / (eigenvalues[:, None] + damping)).astype(jnp.bfloat16)


def tally_scores(grads_got, inputs_got, preconditioned, doc_starts, doc_ends):
    blocks, total_rows, rows_out = grads_got.shape
    queries = preconditioned.shape[1]
    row_step = math.gcd(1024, total_rows)
    flat_pre = preconditioned.reshape(blocks, queries * rows_out, preconditioned.shape[3])

    def one_piece(running, piece_index):
        start_row = piece_index * row_step
        grads_piece = lax.dynamic_slice_in_dim(grads_got, start_row, row_step, 1)
        inputs_piece = lax.dynamic_slice_in_dim(inputs_got, start_row, row_step, 1)
        projected = jnp.einsum(
            "bti,bpi->btp", inputs_piece, flat_pre, preferred_element_type=jnp.float32
        )
        projected = projected.reshape(blocks, row_step, queries, rows_out)
        scores = jnp.sum(projected * grads_piece[:, :, None, :].astype(jnp.float32), axis=(0, 3))
        positions = start_row + lax.iota(jnp.int32, row_step)
        member = (
            (positions[:, None] >= doc_starts[None, :]) & (positions[:, None] < doc_ends[None, :])
        ).astype(jnp.float32)
        added = jnp.einsum("td,tq->dq", member, scores, precision=lax.Precision.HIGHEST)
        return (running + added, None)

    initial = jnp.zeros((doc_starts.shape[0], queries), jnp.float32)
    summed, _ = lax.scan(one_piece, initial, jnp.arange(total_rows // row_step, dtype=jnp.int32))
    return summed


def local_general(
    layer_inputs, output_grads, query_grads, eigenvalues, out_basis, in_basis, doc_lengths
):
    block_width = out_basis.shape[1]
    tok_count = layer_inputs.shape[0]
    tile_count = query_grads.shape[0]
    rows_out = query_grads.shape[2]
    rows_in = query_grads.shape[3]
    in_tiles = layer_inputs.shape[1] // rows_in
    out_tiles = output_grads.shape[1] // rows_out
    tile_ids = lax.axis_index("dp") * tile_count + lax.iota(jnp.int32, tile_count)
    out_sets = out_basis.reshape(out_tiles, rows_out // block_width, block_width, block_width)
    in_sets = in_basis.reshape(in_tiles, rows_in // block_width, block_width, block_width)
    tile_out = jnp.take(out_sets, tile_ids // in_tiles, axis=0)
    tile_in = jnp.take(in_sets, tile_ids % in_tiles, axis=0)
    eigen_sum = lax.psum(jnp.sum(eigenvalues), "dp")
    entries = output_grads.shape[1] * layer_inputs.shape[1]
    damping = 0.1 * (eigen_sum / entries)
    preconditioned = precondition(query_grads, eigenvalues, damping, tile_out, tile_in)
    grads_local = turn_rows(output_grads, out_basis)
    inputs_local = turn_rows(layer_inputs, in_basis)
    grads_tiles = grads_local.reshape(tok_count, out_tiles, rows_out).transpose(1, 0, 2)[:, None]
    grads_tiles = jnp.broadcast_to(grads_tiles, (out_tiles, in_tiles, tok_count, rows_out))
    grads_tiles = grads_tiles.reshape(out_tiles * in_tiles, tok_count, rows_out)
    inputs_tiles = inputs_local.reshape(tok_count, in_tiles, rows_in).transpose(1, 0, 2)[None]
    inputs_tiles = jnp.broadcast_to(inputs_tiles, (out_tiles, in_tiles, tok_count, rows_in))
    inputs_tiles = inputs_tiles.reshape(out_tiles * in_tiles, tok_count, rows_in)
    grads_got, inputs_got = (
        lax.all_to_all(grads_tiles, "dp", split_axis=0, concat_axis=1, tiled=True),
        lax.all_to_all(inputs_tiles, "dp", split_axis=0, concat_axis=1, tiled=True),
    )
    doc_ends = jnp.cumsum(doc_lengths)
    doc_starts = doc_ends - doc_lengths
    partial_scores = tally_scores(grads_got, inputs_got, preconditioned, doc_starts, doc_ends)
    return lax.psum_scatter(partial_scores, "dp", scatter_dimension=0, tiled=True)


def dot_tt(a, b):
    return lax.dot_general(a, b, (((0,), (1,)), ((), ())), preferred_element_type=F32)


def call(body, cost=1, **kw):
    return pl.pallas_call(
        body,
        compiler_params=pltpu.CompilerParams(vmem_limit_bytes=VMEM_LIMIT),
        cost_estimate=pl.CostEstimate(flops=cost, bytes_accessed=1, transcendentals=0),
        **kw,
    )


def in_hbm(value):
    return pltpu.with_memory_space_constraint(value, pltpu.HBM)


def rotate(output_grads, out_basis, chip, chips, layouts, after=(), cost=1):
    tokens, units = output_grads.shape
    width = out_basis.shape[1]
    part = units // chips
    per = part // width
    offsets = [k for layout in layouts for k in layout]
    count = len(offsets)

    def body(chip_ref, g_hbm, b_hbm, *refs):
        o_refs = refs[len(after) : len(after) + len(layouts)]
        g_all, b_all, g_sems, b_sems = refs[len(after) + len(layouts) :]
        copies = []
        for n, k in enumerate(offsets):
            place = chip_ref[0] ^ k
            cols = pl.ds(pl.multiple_of(place * part, part), part)
            blocks = pl.ds(place * per, per)
            copies.append(
                (
                    pltpu.make_async_copy(g_hbm.at[:, cols], g_all.at[n], g_sems.at[n]),
                    pltpu.make_async_copy(b_hbm.at[blocks], b_all.at[n], b_sems.at[n]),
                )
            )
        for pair in copies:
            for copy in pair:
                copy.start()
        n = 0
        for o_ref, layout in zip(o_refs, layouts):
            for top in range(len(layout)):
                for copy in copies[n]:
                    copy.wait()
                for i in range(per):
                    span = slice(i * width, (i + 1) * width)
                    first = top * part + i * width
                    turned = jnp.dot(g_all[n, :, span], b_all[n, i], preferred_element_type=F32)
                    o_ref[first : first + width, :] = turned.astype(BF16).T
                n += 1

    hbm = pl.BlockSpec(memory_space=pl.ANY)
    vmem = pl.BlockSpec(memory_space=pltpu.VMEM)
    return call(
        body,
        cost=cost,
        in_specs=[pl.BlockSpec(memory_space=pltpu.SMEM), hbm, hbm] + [hbm] * len(after),
        out_specs=[vmem] * len(layouts),
        out_shape=[jax.ShapeDtypeStruct((part * len(l), tokens), BF16) for l in layouts],
        scratch_shapes=[
            pltpu.VMEM((count, tokens, part), BF16),
            pltpu.VMEM((count, per, width, width), BF16),
            pltpu.SemaphoreType.DMA((count,)),
            pltpu.SemaphoreType.DMA((count,)),
        ],
        name="rotate",
    )(chip[None], in_hbm(output_grads), in_hbm(out_basis), *after)


def turn(x_ref, first, tokens, basis_ref, o_ref, left=0, cut=None, rest_ref=None):
    count, width, _ = basis_ref.shape
    for i in range(count):
        span = slice(i * width, (i + 1) * width)
        turned = jnp.dot(
            x_ref[first : first + tokens, span], basis_ref[i], preferred_element_type=F32
        )
        turned = turned.astype(BF16).T
        if cut is None or i * width < cut:
            o_ref[span, left : left + tokens] = turned
        else:
            rest_ref[i * width - cut : (i + 1) * width - cut, :] = turned


def turn_inputs(arrays, in_basis):
    count, width, _ = in_basis.shape
    tokens = arrays[0].shape[0]

    def body(*refs):
        for n in range(len(arrays)):
            turn(refs[n], 0, tokens, refs[len(arrays)], refs[len(arrays) + 1 + n])

    vmem = pl.BlockSpec(memory_space=pltpu.VMEM)
    return call(
        body,
        in_specs=[vmem] * (len(arrays) + 1),
        out_specs=[vmem] * len(arrays),
        out_shape=[jax.ShapeDtypeStruct((count * width, tokens), BF16)] * len(arrays),
        name="turn_inputs",
    )(*arrays, in_basis)


def pair_up(a, b, held, after):
    def body(a_ref, b_ref, *refs):
        o_ref = refs[1 + len(after)]
        o_ref[: a.shape[0], :] = a_ref[...]
        o_ref[a.shape[0] :, :] = b_ref[...]

    anywhere = pl.BlockSpec(memory_space=pl.ANY)
    vmem = pl.BlockSpec(memory_space=pltpu.VMEM)
    return call(
        body,
        in_specs=[vmem, vmem] + [anywhere] * (1 + len(after)),
        out_specs=[vmem, anywhere],
        out_shape=[
            jax.ShapeDtypeStruct((a.shape[0] + b.shape[0], a.shape[1]), a.dtype),
            jax.ShapeDtypeStruct(held.shape, held.dtype),
        ],
        input_output_aliases={2: 1},
        name="pair_up",
    )(a, b, held, *after)


def pack_grads(near, far, across):
    part, tokens = near.shape

    def body(n_ref, f_ref, a_ref, near_ref, far_ref, sems):
        top, low = pl.ds(0, part), pl.ds(part, part)
        copies = [
            pltpu.make_async_copy(n_ref, near_ref.at[top], sems.at[0]),
            pltpu.make_async_copy(a_ref.at[low], near_ref.at[low], sems.at[1]),
            pltpu.make_async_copy(f_ref, far_ref.at[top], sems.at[2]),
            pltpu.make_async_copy(a_ref.at[pl.ds(2 * part, part)], far_ref.at[low], sems.at[3]),
        ]
        for copy in copies:
            copy.start()
        for copy in copies:
            copy.wait()

    anywhere = pl.BlockSpec(memory_space=pl.ANY)
    vmem = pl.BlockSpec(memory_space=pltpu.VMEM)
    return call(
        body,
        in_specs=[anywhere] * 3,
        out_specs=[vmem] * 2,
        out_shape=[jax.ShapeDtypeStruct((2 * part, tokens), BF16)] * 2,
        scratch_shapes=[pltpu.SemaphoreType.DMA((4,))],
        name="pack_grads",
    )(near, far, across)


def last_round(x, middle, in_basis, cut, after):
    tokens = x.shape[0]
    count, width, _ = in_basis.shape
    features = count * width
    part = middle.shape[0] // 2

    def body(x_ref, m_ref, b_ref, *refs):
        high_ref, low_ref, sem = refs[len(after) :]
        copy = pltpu.make_async_copy(
            m_ref.at[pl.ds(part, part)], low_ref.at[pl.ds(features - cut, part)], sem
        )
        copy.start()
        turn(x_ref, 0, tokens, b_ref, high_ref, 0, cut, low_ref)
        copy.wait()

    anywhere = pl.BlockSpec(memory_space=pl.ANY)
    vmem = pl.BlockSpec(memory_space=pltpu.VMEM)
    return call(
        body,
        cost=COST_K3,
        in_specs=[vmem, anywhere, vmem] + [anywhere] * len(after),
        out_specs=[vmem] * 2,
        out_shape=[
            jax.ShapeDtypeStruct((cut, tokens), BF16),
            jax.ShapeDtypeStruct((features - cut + part, tokens), BF16),
        ],
        scratch_shapes=[pltpu.SemaphoreType.DMA],
        name="last_round",
    )(x, middle, in_basis, *after)


def sum_eigenvalues(eigenvalues):
    tiles, rows, cols = eigenvalues.shape

    def body(e_ref, o_ref):
        @pl.when(pl.program_id(0) == 0)
        def _():
            o_ref[...] = jnp.zeros_like(o_ref)

        part = jnp.sum(e_ref[0].reshape(rows // 8, 8, cols), axis=0)
        total = part[:, :128]
        for n in range(1, cols // 128):
            total = total + part[:, n * 128 : (n + 1) * 128]
        o_ref[...] += total

    return call(
        body,
        grid=(tiles,),
        in_specs=[pl.BlockSpec((1, rows, cols), lambda b: (b, 0, 0))],
        out_specs=pl.BlockSpec((8, 128), lambda b: (0, 0)),
        out_shape=jax.ShapeDtypeStruct((8, 128), F32),
        name="sum_eigenvalues",
    )(eigenvalues)


def hold(value, *after):
    def body(v_ref, *refs):
        refs[-1][...] = v_ref[...]

    vmem = pl.BlockSpec(memory_space=pltpu.VMEM)
    return call(
        body,
        in_specs=[vmem] + [pl.BlockSpec(memory_space=pl.ANY)] * len(after),
        out_specs=vmem,
        out_shape=jax.ShapeDtypeStruct(value.shape, value.dtype),
        name="hold",
    )(value, *after)


def block_diagonal(blocks):
    count, width = len(blocks), blocks[0].shape[0]
    zero = jnp.zeros((width, width), blocks[0].dtype)
    rows = [
        jnp.concatenate([blocks[i] if i == j else zero for j in range(count)], axis=1)
        for i in range(count)
    ]
    return jnp.concatenate(rows, axis=0)


def precondition_rows(query_grads, eigenvalues, sums, out_basis, in_basis, me, entries, after):
    tiles, queries, rows, cols = query_grads.shape
    width = in_basis.shape[1]
    features = in_basis.shape[0] * width
    in_tiles = features // cols
    groups = tiles // in_tiles
    n_out, n_in = rows // width, cols // width
    pair = 2 if n_out % 2 == 0 else 1
    span = pair * width

    def body(me_ref, q_ref, e_ref, s_ref, ob_ref, ib_ref, *refs):
        o_ref, turn_ref = refs[len(after) :]

        @pl.when(pl.program_id(0) % in_tiles == 0)
        def _():
            for n in range(n_out // pair):
                turn_ref[n] = block_diagonal([ob_ref[n * pair + k].T for k in range(pair)])

        damping = 0.1 * (jnp.sum(s_ref[...], keepdims=True) / entries)
        scale = 1.0 / (e_ref[0] + damping)
        half = jnp.dot(
            q_ref[0].reshape(queries * rows, cols),
            block_diagonal([ib_ref[n] for n in range(n_in)]),
            preferred_element_type=F32,
        ).astype(BF16)
        for q in range(queries):
            for n in range(n_out // pair):
                start = n * span
                turned = jnp.dot(
                    turn_ref[n],
                    half[q * rows + start : q * rows + start + span],
                    preferred_element_type=F32,
                )
                o_ref[q, start : start + span, :] = (turned * scale[start : start + span]).astype(
                    BF16
                )

    grid_spec = pltpu.PrefetchScalarGridSpec(
        num_scalar_prefetch=1,
        grid=(tiles,),
        in_specs=[
            pl.BlockSpec((1, queries, rows, cols), lambda b, m: (b, 0, 0, 0)),
            pl.BlockSpec((1, rows, cols), lambda b, m: (b, 0, 0)),
            pl.BlockSpec(sums.shape, lambda b, m: (0, 0)),
            pl.BlockSpec((n_out, width, width), lambda b, m: (m[0] * groups + b // in_tiles, 0, 0)),
            pl.BlockSpec((n_in, width, width), lambda b, m: (b % in_tiles, 0, 0)),
        ]
        + [pl.BlockSpec(memory_space=pl.ANY)] * len(after),
        out_specs=pl.BlockSpec(
            (queries, rows, cols), lambda b, m: (0, b // in_tiles, b % in_tiles)
        ),
        scratch_shapes=[pltpu.VMEM((n_out // pair, span, span), BF16)],
    )
    return call(
        body,
        grid_spec=grid_spec,
        out_shape=jax.ShapeDtypeStruct((queries, groups * rows, features), BF16),
        name="precondition",
        cost=COST_PRE,
    )(me[None], query_grads, eigenvalues, sums, out_basis, in_basis, *after)


def join_and_tally(where, turned_piece, pieces, early, in_basis, own, sibling, starts, ends, order):
    queries, rows, features = own.shape
    docs, tokens = starts.shape
    width = in_basis.shape[1]
    block = math.gcd(rows, 256)
    all_pieces = [turned_piece] + list(pieces)
    count = len(all_pieces)
    raw = [x for x, _ in pieces] + list(early)
    ready = [x.shape[0] == features for x, _ in raw]
    cut = turned_piece[0][0].shape[0]
    raw_place = [next(i for i, o in enumerate(order) if o is x) for x, _ in raw]
    heights = [0 if a.shape[0] == features else a.shape[0] for a in order]
    tops = [sum(heights[:i]) for i in range(len(heights))]
    grads = [g for _, (g, _) in all_pieces]
    operands = [in_hbm(a) for a in order] + [in_hbm(in_basis), *turned_piece[0]]
    operands += [in_hbm(g) for g in grads] + [own, sibling, starts, ends]

    def body(where_ref, *refs):
        raw_refs = refs[: len(order)]
        basis_hbm, high_hbm, low_hbm = refs[len(order) : len(order) + 3]
        g_hbm = refs[len(order) + 3 : len(order) + 3 + count]
        own_ref, sib_ref, st_ref, en_ref, o_ref, both_ref = refs[
            len(order) + 3 + count : len(operands) + 2
        ]
        t_refs = refs[len(operands) + 2 : -7]
        raw_all, basis_ref, x_all, g_all, x_sems, g_sems, p_sems = refs[-7:]
        x_copies = [pltpu.make_async_copy(basis_hbm, basis_ref, x_sems.at[len(order)])]
        for n, i in enumerate(raw_place):
            if ready[n]:
                place = x_all.at[:, pl.ds((n + 1) * tokens, tokens)]
                x_copies.append(pltpu.make_async_copy(raw_refs[i], place, x_sems.at[i]))
        for i in range(len(order)):
            if heights[i]:
                place = raw_all.at[pl.ds(tops[i], heights[i])]
                x_copies.append(pltpu.make_async_copy(raw_refs[i], place, x_sems.at[i]))
        copies = [
            [
                pltpu.make_async_copy(p_ref.at[q], both_ref.at[c, q], p_sems.at[c, q])
                for q in range(queries)
            ]
            for c, p_ref in enumerate((own_ref, sib_ref))
        ]
        x_copies += [
            pltpu.make_async_copy(
                high_hbm, x_all.at[pl.ds(0, cut), pl.ds(0, tokens)], x_sems.at[len(order) + 1]
            ),
            pltpu.make_async_copy(
                low_hbm.at[pl.ds(0, features - cut)],
                x_all.at[pl.ds(cut, features - cut), pl.ds(0, tokens)],
                x_sems.at[len(order) + 2],
            ),
        ]
        g_copies = [
            pltpu.make_async_copy(
                g_hbm[n].at[pl.ds(all_pieces[n][1][1], 2 * rows)], g_all.at[n], g_sems.at[n]
            )
            for n in range(count)
        ]
        for copy in x_copies:
            copy.start()
        copies[0][0].start()
        for copy in g_copies:
            copy.start()
        for c in range(2):
            for q in range(queries):
                if c or q:
                    copies[c][q].start()
        for copy in x_copies:
            copy.wait()
        for n, (_, first) in enumerate(raw):
            if ready[n]:
                continue
            turn(raw_all, tops[raw_place[n]] + first, tokens, basis_ref, x_all, (n + 1) * tokens)
        scores = [[jnp.zeros((1, tokens), F32)] * queries for _ in all_pieces]
        for c in range(2):
            core = where_ref[0] if c == 0 else 1 - where_ref[0]
            for q in range(queries):
                copies[c][q].wait()
                if c == 0 and q == 0:
                    for copy in g_copies:
                        copy.wait()
                for r in range(0, rows, block):
                    turned = jnp.dot(
                        both_ref[c, q, r : r + block, :], x_all[...], preferred_element_type=F32
                    )
                    for n, t_ref in enumerate(t_refs):
                        left = (count + n) * tokens
                        t_ref[c, q, r : r + block, :] = turned[:, left : left + tokens]
                    for n in range(count):
                        spot = pl.ds(pl.multiple_of(core * rows + r, block), block)
                        scores[n][q] = scores[n][q] + jnp.sum(
                            turned[:, n * tokens : (n + 1) * tokens]
                            * g_all[n, spot, :].astype(F32),
                            axis=0,
                            keepdims=True,
                        )
        add_shares(where_ref, scores, None, st_ref, en_ref, o_ref)

    hbm = pl.BlockSpec(memory_space=pl.ANY)
    vmem = pl.BlockSpec(memory_space=pltpu.VMEM)
    kept = jax.ShapeDtypeStruct((2, queries, rows, tokens), F32)
    return call(
        body,
        in_specs=[pl.BlockSpec(memory_space=pltpu.SMEM)]
        + [hbm] * (len(order) + 3 + count)
        + [hbm, hbm, vmem, vmem],
        out_specs=[vmem] * (2 + len(early)),
        out_shape=[
            jax.ShapeDtypeStruct((queries, docs, tokens), F32),
            jax.ShapeDtypeStruct((2,) + own.shape, own.dtype),
        ]
        + [kept] * len(early),
        scratch_shapes=[
            pltpu.VMEM((sum(heights), features), BF16),
            pltpu.VMEM(in_basis.shape, BF16),
            pltpu.VMEM((features, (count + len(early)) * tokens), BF16),
            pltpu.VMEM((count, 2 * rows, tokens), BF16),
            pltpu.SemaphoreType.DMA((len(order) + 3,)),
            pltpu.SemaphoreType.DMA((count,)),
            pltpu.SemaphoreType.DMA((2, queries)),
        ],
        name="join_and_tally",
    )(where, *operands)


def add_shares(where_ref, scores, run_ref, st_ref, en_ref, o_ref):
    docs, tokens = st_ref.shape
    for q in range(len(scores[0])):
        total = jnp.zeros((docs, tokens), F32) if run_ref is None else run_ref[q]
        for n in range(len(scores)):
            spot = where_ref[1 + n] * tokens + lax.broadcasted_iota(jnp.int32, (docs, tokens), 1)
            inside = (spot >= st_ref[...]) & (spot < en_ref[...])
            total = total + jnp.where(inside, scores[n][q], 0.0)
        o_ref[q] = total


def project(inputs, rows_of, both, after, base=None):
    cores, queries, rows, features = both.shape
    tokens = inputs.shape[1]
    first, end = rows_of
    block = math.gcd(rows, 512)
    bases = [] if base is None else [base]

    def body(x_ref, p_ref, *refs):
        for c in range(cores):
            for q in range(queries):
                for r in range(0, rows, block):
                    span = slice(r, r + block)
                    turned = jnp.dot(
                        p_ref[c, q, span, first:end],
                        x_ref[: end - first, :],
                        preferred_element_type=F32,
                    )
                    refs[-1][c, q, span, :] = refs[0][c, q, span, :] + turned if bases else turned

    vmem = pl.BlockSpec(memory_space=pltpu.VMEM)
    return call(
        body,
        in_specs=[vmem] * (2 + len(bases)) + [pl.BlockSpec(memory_space=pl.ANY)] * len(after),
        out_specs=vmem,
        out_shape=jax.ShapeDtypeStruct((cores, queries, rows, tokens), F32),
        name="project",
    )(inputs, both, *bases, *after)


def tally(where, projected, grads, starts, ends, running, order):
    cores, queries, rows, tokens = projected[0].shape
    block = math.gcd(rows, 512)
    arrays = list(order)
    places = [next(i for i, o in enumerate(arrays) if o is array) for array, _ in grads]
    held = len(projected)

    def body(where_ref, *refs):
        g_refs = refs[held : held + len(arrays)]
        st_ref, en_ref, run_ref, o_ref = refs[held + len(arrays) :]
        scores = [[jnp.zeros((1, tokens), F32)] * queries for _ in grads]
        for c in range(cores):
            core = where_ref[0] if c == 0 else 1 - where_ref[0]
            for q in range(queries):
                for r in range(0, rows, block):
                    for n, (_, first) in enumerate(grads):
                        spot = pl.ds(pl.multiple_of(core * rows + first + r, block), block)
                        scores[n][q] = scores[n][q] + jnp.sum(
                            refs[n][c, q, r : r + block, :]
                            * g_refs[places[n]][spot, :].astype(F32),
                            axis=0,
                            keepdims=True,
                        )
        add_shares(where_ref, scores, run_ref, st_ref, en_ref, o_ref)

    vmem = pl.BlockSpec(memory_space=pltpu.VMEM)
    return call(
        body,
        in_specs=[pl.BlockSpec(memory_space=pltpu.SMEM)] + [vmem] * (held + len(arrays) + 3),
        out_specs=vmem,
        out_shape=jax.ShapeDtypeStruct(running.shape, F32),
        name="tally",
    )(where, *projected, *arrays, starts, ends, running)


def local_rows(
    depth, layer_inputs, output_grads, query_grads, eigenvalues, out_basis, in_basis, doc_lengths
):
    devices = 4 * depth
    chips = 2 * depth
    tokens = layer_inputs.shape[0]
    queries = query_grads.shape[1]
    entries = output_grads.shape[1] * layer_inputs.shape[1]
    me = lax.axis_index("dp")
    chip = me // 2
    core = me % 2

    def swap(value, offset):
        return lax.ppermute(value, "dp", [(i, i ^ offset) for i in range(devices)])

    features = layer_inputs.shape[1]
    part = output_grads.shape[1] // chips
    spin = functools.partial(rotate, output_grads, out_basis, chip, chips)
    far_x = swap(layer_inputs, 12)
    near_x = swap(layer_inputs, 4)
    side_x = swap(layer_inputs, 2)
    sums = sum_eigenvalues(eigenvalues)
    (side_g,) = spin([[1, 3, 7]], [sums], cost=COST_K1)
    side_g = swap(side_g, 2)

    g_own, middle, g_far, near_g = spin([[0], [4, 5], [6], [2]], cost=COST_KG)
    sums = sums + swap(sums, 2)
    sums = hold(sums, middle)
    for offset in (1, 4):
        sums = sums + swap(sums, offset)

    sides_sent, middle = pair_up(near_x, far_x, middle, [side_x])
    middle = swap(middle, 8)
    middle_x = swap(far_x, 4)
    sides = swap(sides_sent, 2)

    sums = hold(sums, sides_sent)
    sums = sums + swap(sums, 8)
    own = precondition_rows(
        query_grads, eigenvalues, sums, out_basis, in_basis, me, entries, [near_x, far_x, side_x, side_g]
    )
    sibling = swap(own, 1)

    near_g, g_far = pack_grads(near_g, g_far, side_g)
    near_g = swap(near_g, 4)
    g_far = swap(g_far, 12)
    cut = features * 7 // 8
    x0, x1, x2, x6 = turn_inputs([layer_inputs, side_x, near_x, far_x], in_basis)
    turned = last_round(middle_x, middle, in_basis, cut, [sides, own, x0])
    high, low = [swap(value, 2) for value in turned]

    doc_ends = jnp.cumsum(doc_lengths)
    doc_starts = doc_ends - doc_lengths
    docs = doc_lengths.shape[0]
    starts = jnp.broadcast_to(doc_starts[:, None], (docs, tokens))
    ends = jnp.broadcast_to(doc_ends[:, None], (docs, tokens))

    def where(*offsets):
        return jnp.stack([core] + [me ^ (2 * k) for k in offsets]).astype(jnp.int32)

    running, both, *kept = join_and_tally(
        where(4, 0, 1),
        (turned, (middle, 0)),
        [((x0, 0), (g_own, 0)), ((x1, 0), (side_g, 0))],
        [(x2, 0), (sides, 0), (x6, 0), (sides, tokens)],
        in_basis,
        own,
        sibling,
        starts,
        ends,
        [x0, x1, x2, x6, sides],
    )
    part_way = project(high, (0, cut), both, [running])
    kept.append(project(low, (cut, features), both, [], part_way))
    running = tally(
        where(2, 3, 6, 7, 5),
        kept,
        [(near_g, 0), (near_g, part), (g_far, 0), (g_far, part), (low, features - cut)],
        starts,
        ends,
        running,
        [near_g, g_far, low],
    )
    shares = jnp.sum(running, axis=2)
    for offset in (1, 2, 4, 8):
        shares = shares + swap(shares, offset)
    each = docs // devices
    mine = lax.dynamic_slice_in_dim(shares, me * each, each, 1)
    return mine.T


def local(layer_inputs, output_grads, query_grads, eigenvalues, out_basis, in_basis, doc_lengths, devices):
    args = (layer_inputs, output_grads, query_grads, eigenvalues, out_basis, in_basis, doc_lengths)
    in_tiles = layer_inputs.shape[1] // query_grads.shape[3]
    tile_count = query_grads.shape[0]
    if devices == 16 and tile_count % in_tiles == 0:
        return local_rows(devices // 4, *args)
    return local_general(*args)


def solution(mesh):
    in_specs = (
        P(("groups", "dp"), None),
        P(("groups", "dp"), None),
        P("dp", None, None, None),
        P("dp", None, None),
        P(),
        P(),
        P("groups"),
    )
    out_specs = P(("groups", "dp"), None)
    body = functools.partial(local, devices=mesh.shape["dp"])
    return jax.shard_map(body, mesh=mesh, in_specs=in_specs, out_specs=out_specs, check_vma=False)
```
